256 devices in a mesh: curve: 64 (over x, z, core), field: 4 (over y).
Axes of the slice: x: 4, y: 4, z: 8, core: 2. Of those that a mesh axis runs over, the one named last changes fastest.
Arguments:
- column_state: float32 [72, 48, 4096], P(None, 'field', 'curve'), may hold values from -6 to 6
- span_of: int32 [4096], P('curve'), may hold values from 0 to 63, as said below
- diffusivity: float32 [72, 8192], P(None, 'curve'), may hold values from 0.02 to 20
- courant: float32 [72, 8192], P(None, 'curve'), may hold values from 0.05 to 0.9
- cloud_levels: int32 [8192], P('curve'), may hold values from 1 to 72
- neighbors: int32 [4, 256], P(None, 'curve'), may hold values from 0 to 255, as said below
Outputs:
- span_state: float32 [72, 48, 8192], P(None, 'field', 'curve')
- dynamics_state: float32 [72, 48, 4096], P(None, 'field', 'curve')
The draws below stay inside these ranges and needn't reach their ends.
Inputs may be any that keep to these rules, and one draw needn't show every extreme that they name: `span_of`: from the columns of one block at most 2 go to one span; in every draw one span receives exactly 2 columns from every block. `neighbors`: edges pair up: if element f lies across edge s of element g, then g lies across edge (s + 2) % 4 of f. Every neighbour lies in the same block of 4 elements as the element, or in the block just before or just after it along the curve, the last block being followed by the first.
All inputs are finite; a program needn't handle non-finite values.
Results may differ from the reference program's by a relative error of at most 0.00007.
Values sent between devices are 32-bit elements; how exact they have to be, the bound alone decides.
No kernel may reach another device: no remote copies, remote signals or barrier semaphores. Data moves between devices by JAX's collectives and lax.ppermute only.
A program may use at most 128 MiB of HBM per device.

```python
import math
import jax
import jax.numpy as jnp
import numpy as np
from jax import lax

LEV = 72
NF = 48
COL_DEV = 64
E_DEV = 4
CAP = 2
SLOT_DEV = 128
COLS = 4096
SLOTS = 8192
ELEMS = 256


def draw_span_of(key, part):
    key = jax.random.fold_in(key, 3)
    first_key, second_key = jax.random.split(key)
    sources = COLS // COL_DEV
    busiest = jax.random.randint(first_key, (), 0, sources)
    span_pool = jnp.arange((sources - 1) * CAP, dtype=jnp.int32) // CAP
    span_pool = span_pool + (span_pool >= busiest).astype(jnp.int32)

    def one_block(subkey):
        pick_key, order_key = jax.random.split(subkey)
        chosen = jax.random.permutation(pick_key, span_pool)[:COL_DEV - CAP]
        assigned = jnp.concatenate([chosen, jnp.zeros((CAP,), jnp.int32) + busiest])
        return jax.random.permutation(order_key, assigned)
    return jax.vmap(one_block)(jax.random.split(second_key, sources)).reshape(-1).astype(jnp.int32)


def edge_pairing(subkey):
    blocks = ELEMS // E_DEV
    flow_key, send_key, recv_key = jax.random.split(subkey, 3)
    flow = jax.random.randint(flow_key, (blocks,), 1, E_DEV // 2 + 1).astype(jnp.int32)
    flow = flow.at[0].set(E_DEV // 2)
    send_perm = jax.vmap(lambda inner: jax.random.permutation(inner, E_DEV))(jax.random.split(send_key, blocks)).astype(jnp.int32)
    recv_perm = jax.vmap(lambda inner: jax.random.permutation(inner, E_DEV))(jax.random.split(recv_key, blocks)).astype(jnp.int32)
    block_ids = jnp.arange(blocks, dtype=jnp.int32)[:, None]
    upward = flow[:, None]
    downward = jnp.roll(flow, 1)[:, None]
    before_prior = jnp.roll(flow, 2)[:, None]
    order = jnp.arange(E_DEV, dtype=jnp.int32)[None, :]
    go_up = order < upward
    go_down = jnp.logical_and(order >= upward, order < upward + downward)
    target_block = jnp.where(go_up, (block_ids + 1) % blocks, jnp.where(go_down, (block_ids + blocks - 1) % blocks, block_ids + 0 * order))
    target_slot = jnp.where(go_up, order, jnp.where(go_down, before_prior + order - upward, order))
    target = target_block * E_DEV + jnp.take(recv_perm.reshape(-1), target_block * E_DEV + target_slot)
    anchor = (block_ids * E_DEV + send_perm).reshape(-1)
    target = target.reshape(-1).astype(jnp.int32)
    forward = jnp.zeros((ELEMS,), jnp.int32).at[anchor].set(target)
    backward = jnp.zeros((ELEMS,), jnp.int32).at[target].set(anchor)
    return (forward, backward)


def draw_neighbors(key, part):
    key = jax.random.fold_in(key, 7)
    north_key, east_key = jax.random.split(key)
    north, south = edge_pairing(north_key)
    east, west = edge_pairing(east_key)
    return jnp.stack([south, east, north, west]).astype(jnp.int32)


def touch_ends(drawn, rng, low, largest):
    place = [jax.random.randint(jax.random.fold_in(rng, axis), (), 0, length) for axis, length in enumerate(drawn.shape)]
    main_axis = drawn.shape.index(max(drawn.shape))
    neighbour = place[:main_axis] + [(place[main_axis] + 1) % drawn.shape[main_axis]] + place[main_axis + 1:]
    return drawn.at[tuple(place)].set(low).at[tuple(neighbour)].set(largest)


def block_scale(own_key, shape, cuts, smallest, largest):
    def one(axis_at, parts):
        steps = jax.random.uniform(jax.random.fold_in(jax.random.fold_in(own_key, 6), axis_at), (parts,), jnp.float32, smallest / len(cuts), largest / len(cuts))
        return jnp.repeat(jnp.exp(steps), shape[axis_at] // parts).reshape((-1,) + (1,) * (len(shape) - axis_at - 1))

    factor_of = one(*cuts[0])
    for cut in cuts[1:]:
        factor_of = factor_of * one(*cut)
    return factor_of


def centred(key, dims, spread, limit, cuts=(), held_as=jnp.bfloat16):
    drawn = jax.random.normal(key, dims, jnp.float32) * spread
    if len(cuts) > 0:
        drawn = block_scale(key, dims, cuts, -0.22, 0.18) * drawn
    return jnp.clip(drawn, min=-limit, max=limit).astype(held_as)


def setup_inputs(seed: int = 0) -> dict:
    streams_of = jax.random.split(jax.random.key(seed), 7)
    column_state = centred(streams_of[0], (LEV, NF, COLS), 1.0, 6.0, ((1, 4), (2, 64)), jnp.float32)
    span_of = draw_span_of(jax.random.fold_in(streams_of[6], 71), 0)
    diffusivity = jnp.clip(jnp.exp(math.log(20.0) - 6.9077553 * jax.random.uniform(streams_of[2], (LEV, SLOTS), jnp.float32) ** block_scale(streams_of[2], (LEV, SLOTS), ((1, 64),), -0.2, 0.2)), 0.02, 20.0)
    courant = jnp.clip(0.05 + 0.84999998 * jax.random.uniform(streams_of[3], (LEV, SLOTS), jnp.float32) ** block_scale(streams_of[3], (LEV, SLOTS), ((1, 64),), -0.2, 0.2), 0.05, 0.9)
    cloud_levels = touch_ends(jax.random.randint(streams_of[4], (SLOTS,), 1, LEV + 1), jax.random.fold_in(streams_of[4], 1), 1, LEV).astype(jnp.int32)
    neighbors = draw_neighbors(jax.random.fold_in(streams_of[6], 71), 0)
    return dict(column_state=column_state, span_of=span_of, diffusivity=diffusivity, courant=courant, cloud_levels=cloud_levels, neighbors=neighbors)


viscosity = 0.02
edge_table = np.array([[0, 1, 2, 3], [3, 7, 11, 15], [15, 14, 13, 12], [12, 8, 4, 0]])
opposite = np.array([2, 3, 0, 1])
scatter_table = (np.arange(16)[:, None, None] == edge_table[None, :, :]).astype(np.float32)
second_diff = np.array([[-1.0, 1.0, 0.0, 0.0], [1.0, -2.0, 1.0, 0.0], [0.0, 1.0, -2.0, 1.0], [0.0, 0.0, 1.0, -1.0]])
lap_table = np.kron(np.eye(4), second_diff) + np.kron(second_diff, np.eye(4))


def level_factors(coefficients):
    zero_row = jnp.zeros_like(coefficients[0])

    def sweep(carried, coef_here):
        coef_above, ratio_above = carried
        inverse = 1.0 / (1.0 + coef_above + coef_here - coef_above * ratio_above)
        ratio_here = coef_here * inverse
        return (coef_here, ratio_here), (inverse, ratio_here, coef_above)

    _, factors = lax.scan(sweep, (zero_row, zero_row), coefficients)
    return factors


def column_physics(column_state, fall_cols, cloud_cols, factors):
    inverse, sweep_ratio, coef_above = factors
    levels = column_state.shape[0]
    active = jnp.arange(levels, dtype=jnp.int32)[:, None] >= (levels - cloud_cols)[None, :]
    fall_rate = jnp.where(active, fall_cols, jnp.zeros_like(fall_cols))
    fall_flux = fall_rate[:, None, :] * column_state
    from_above = jnp.concatenate([jnp.zeros_like(fall_flux[:1]), fall_flux[:-1]], axis=0)
    settled = column_state - fall_flux + from_above

    def downward(partial_sol, inputs):
        source_row, inverse_row, coef_row = inputs
        partial_sol = (source_row + coef_row[None, :] * partial_sol) * inverse_row[None, :]
        return partial_sol, partial_sol

    _, partials = lax.scan(downward, jnp.zeros_like(settled[0]), (settled, inverse, coef_above))

    def upward(solved, inputs):
        partial_row, ratio_row = inputs
        solved = partial_row + ratio_row[None, :] * solved
        return solved, solved

    _, solution = lax.scan(upward, jnp.zeros_like(settled[0]), (partials, sweep_ratio), reverse=True)
    return solution


def edge_sum(field, neighbors):
    levels, fields, columns = field.shape
    elements = COL_DEV // 16
    blocks = columns // COL_DEV
    arranged = field.reshape(levels, fields, blocks, 16, elements)
    edge_vals = jnp.moveaxis(arranged[:, :, :, edge_table, :], 2, 4).reshape(levels, fields, 4, 4, blocks * elements)
    facing = edge_vals[:, :, opposite, ::-1, :]
    pieces = []
    for side in range(4):
        pieces.append(jnp.take(facing[:, :, side], neighbors[side], axis=-1))
    across = jnp.stack(pieces, axis=2)
    change = 0.5 * (across - edge_vals)
    increment = jnp.einsum("nsp,lfspg->lfng", jnp.asarray(scatter_table, dtype=field.dtype), change, precision=lax.Precision.HIGHEST)
    increment = jnp.moveaxis(increment.reshape(levels, fields, 16, blocks, elements), 3, 2)
    return (arranged + increment).reshape(levels, fields, columns)


def apply_lap(field):
    levels, fields, columns = field.shape
    arranged = field.reshape(levels, fields, columns // COL_DEV, 16, COL_DEV // 16)
    result = jnp.einsum("nm,lfbme->lfbne", jnp.asarray(lap_table, dtype=field.dtype), arranged, precision=lax.Precision.HIGHEST)
    return result.reshape(levels, fields, columns)


def reference(column_state, span_of, diffusivity, courant, cloud_levels, neighbors):
    sources = COLS // COL_DEV
    block_dest = span_of.reshape(sources, COL_DEV)
    onehot = (block_dest[:, :, None] == jnp.arange(sources, dtype=jnp.int32)[None, None, :]).astype(jnp.int32)
    order_rank = jnp.sum(jnp.cumsum(onehot, axis=1) * onehot, axis=2) - 1
    slot_index = (block_dest * SLOT_DEV + jnp.arange(sources, dtype=jnp.int32)[:, None] * CAP + order_rank).reshape(-1).astype(jnp.int32)
    diff_cols = jnp.take(diffusivity, slot_index, axis=1)
    fall_cols = jnp.take(courant, slot_index, axis=1)
    cloud_cols = jnp.take(cloud_levels, slot_index, axis=0)
    physics_state = column_physics(column_state, fall_cols, cloud_cols, level_factors(diff_cols))
    span_state = jnp.zeros((LEV, NF, SLOTS), column_state.dtype).at[:, :, slot_index].set(physics_state)
    smoothed = edge_sum(physics_state, neighbors)
    second = edge_sum(apply_lap(smoothed), neighbors)
    dynamics_state = smoothed - viscosity * apply_lap(second)
    return span_state, dynamics_state
```

```python
import numpy as np
import jax
import jax.numpy as jnp
from jax import lax
from jax.experimental import pallas as pl
from jax.experimental.pallas import tpu as pltpu
from jax.sharding import PartitionSpec as P

LEV = 72
HALF = LEV // 2
NF = 12
PAIR = NF // 2
COL = 64
SLOT = 128
WORDS = 1024
CHUNKS = WORDS // 128
STATE = NF * LEV
SPANS = 64
viscosity = 0.02

second_diff = np.array(
    [[-1.0, 1.0, 0.0, 0.0], [1.0, -2.0, 1.0, 0.0], [0.0, 1.0, -2.0, 1.0], [0.0, 0.0, 1.0, -1.0]]
)
lap_nodes = np.kron(np.eye(4), second_diff) + np.kron(second_diff, np.eye(4))
lap_columns = np.kron(lap_nodes, np.eye(4)).astype(np.float32)

f32 = jnp.float32
bf16 = jnp.bfloat16


def iota(shape, axis):
    return lax.broadcasted_iota(jnp.int32, shape, axis)


def split3(x):
    hi = x.astype(bf16)
    rest = x - hi.astype(f32)
    mid = rest.astype(bf16)
    lo = (rest - mid.astype(f32)).astype(bf16)
    return hi, mid, lo


def split2(x):
    hi = x.astype(bf16)
    return hi, (x - hi.astype(f32)).astype(bf16)


def dot(a, b):
    return jnp.dot(a, b, preferred_element_type=f32)


def slots_of(span_row):
    row = span_row.astype(f32)
    square = jnp.broadcast_to(row, (COL, COL))
    column = jnp.sum(
        jnp.where(iota((COL, COL), 0) == iota((COL, COL), 1), square, 0.0), axis=1, keepdims=True
    )
    earlier = jnp.logical_and(column == square, iota((COL, COL), 0) < iota((COL, COL), 1))
    rank = jnp.sum(jnp.where(earlier, 1.0, 0.0), axis=0, keepdims=True)
    return (2.0 * row + rank).astype(jnp.int32)


def active_rate(courant, cloud_row):
    level = iota((LEV, SLOT), 0)
    return jnp.where(level >= LEV - cloud_row, courant, 0.0)


def pack_kernel(x_ref, span_ref, diff_ref, courant_ref, cloud_ref, near_ref, out_ref, slot_ref):
    slot_row = slots_of(span_ref[...])
    slot_ref[...] = jnp.broadcast_to(jnp.concatenate([slot_row, slot_row], axis=1), (8, SLOT))
    pick = (iota((SLOT, COL), 0) == slot_row).astype(f32).astype(bf16)
    state = jnp.concatenate([x_ref[f] for f in range(NF)], axis=1)
    hi, mid, lo = split3(state)
    packed = dot(pick, hi) + dot(pick, mid) + dot(pick, lo)
    diff_t = diff_ref[...].T
    rate_t = active_rate(courant_ref[...], cloud_ref[...]).T
    near = near_ref[...].astype(f32)
    near_row = jnp.concatenate([near[s : s + 1, :] for s in range(4)], axis=1)
    near_t = jnp.broadcast_to(near_row, (SLOT, 16))
    message = jnp.concatenate([packed, diff_t, rate_t, near_t], axis=1)
    for k in range(CHUNKS):
        out_ref[pl.ds(k, SLOT, stride=CHUNKS), :] = message[:, 128 * k : 128 * k + 128]


def turn_kernel(x_ref, out_ref):
    for f in range(PAIR):
        both = jnp.concatenate([x_ref[f], x_ref[f + PAIR]], axis=0)
        out_ref[pl.ds(f * LEV, LEV), :] = both.T


def chunk_t(recv_ref, k):
    return recv_ref[pl.ds(k, SLOT, stride=CHUNKS), :].T


def solve(coef_ref, rate_ref, groups, part_ref, ratio_ref):
    rows = (PAIR, 128)
    zero = jnp.zeros(rows, f32)

    def row(ref, k):
        return jnp.broadcast_to(ref[pl.ds(k, 1), :], rows)

    count = len(groups)
    top_ratio, bot_ratio = zero, zero
    top_part, bot_part = [zero] * count, [zero] * count
    top_flux = [zero] * count
    top_above = zero
    bot_below = row(coef_ref, LEV - 1)
    last = row(rate_ref, LEV - 1)
    bot_state = [load(LEV - 1) for load, _ in groups]
    bot_flux = [last * x for x in bot_state]
    for i in range(HALF):
        t, u = i, LEV - 1 - i
        top_next = row(coef_ref, t)
        bot_next = row(coef_ref, u - 1)
        top_inv = 1.0 / (1.0 + top_above + top_next - top_above * top_ratio)
        bot_inv = 1.0 / (1.0 + bot_below + bot_next - bot_below * bot_ratio)
        top_ratio = top_next * top_inv
        bot_ratio = bot_next * bot_inv
        ratio_ref[i] = top_ratio
        ratio_ref[HALF + i] = bot_ratio
        top_rate = row(rate_ref, t)
        above_rate = row(rate_ref, u - 1)
        for g, (load, _) in enumerate(groups):
            x = load(t)
            flux = top_rate * x
            settled = x - flux + top_flux[g]
            top_flux[g] = flux
            top_part[g] = (settled + top_above * top_part[g]) * top_inv
            part_ref[g, i] = top_part[g]
            above = load(u - 1)
            above_flux = above_rate * above
            settled = bot_state[g] - bot_flux[g] + above_flux
            bot_state[g] = above
            bot_flux[g] = above_flux
            bot_part[g] = (settled + bot_below * bot_part[g]) * bot_inv
            part_ref[g, HALF + i] = bot_part[g]
        top_above = top_next
        bot_below = bot_next
    meet = 1.0 / (1.0 - top_ratio * bot_ratio)
    top, bot = [], []
    for g, (_, store) in enumerate(groups):
        top.append((top_part[g] + top_ratio * bot_part[g]) * meet)
        bot.append((bot_part[g] + bot_ratio * top_part[g]) * meet)
        store(HALF - 1, top[g])
        store(HALF, bot[g])
    for i in range(HALF - 2, -1, -1):
        top_ratio = ratio_ref[i]
        bot_ratio = ratio_ref[HALF + i]
        for g, (_, store) in enumerate(groups):
            top[g] = part_ref[g, i] + top_ratio * top[g]
            bot[g] = part_ref[g, HALF + i] + bot_ratio * bot[g]
            store(i, top[g])
            store(LEV - 1 - i, bot[g])


def strided(in_ref, out_ref, base):
    def load(level):
        return in_ref[pl.ds(base + level, PAIR, stride=LEV), :]

    def store(level, value):
        out_ref[pl.ds(base + level, PAIR, stride=LEV), :] = value

    return load, store


def element_kernel(recv_ref, slot_ref, x_ref, out_ref, coef_ref, rate_ref, part_ref, ratio_ref):
    spread = (iota((SLOT, 128), 0) == slot_ref[0:1, :]).astype(f32).astype(bf16)
    tail = jnp.concatenate([chunk_t(recv_ref, CHUNKS - 2), chunk_t(recv_ref, CHUNKS - 1)], axis=0)
    begin = STATE - 128 * (CHUNKS - 2)
    hi, mid, lo = split3(tail[begin : begin + 2 * LEV])
    columns = dot(hi, spread) + dot(mid, spread) + dot(lo, spread)
    coef_ref[...] = columns[:LEV]
    rate_ref[...] = columns[LEV:]
    solve(coef_ref, rate_ref, [strided(x_ref, out_ref, 0)], part_ref, ratio_ref)


def halo_matrix(recv_ref, lap_ref, matrix_ref):
    device = lax.axis_index("curve")
    lap = lap_ref[...].astype(bf16)
    lane = iota((1, COL), 1)
    node = lane // 4
    node_row, node_col = node // 4, node % 4
    on_edge = [node_row == 0, node_col == 3, node_row == 3, node_col == 0]
    facing = [node + 12, node - 3, node - 12, node + 3]
    edges = sum(jnp.where(edge, 1.0, 0.0) for edge in on_edge)
    word = iota((128, 4 * COL), 0) - (128 - 16)
    place = iota((128, 4 * COL), 1)
    spread = (word == (place // COL) * 4 + place % 4).astype(f32).astype(bf16)
    rows = []
    for o in range(3):
        block = lax.rem(device + (o - 1) + SPANS, SPANS)
        rows.append(recv_ref[pl.ds(block * 16 + CHUNKS - 1, 1), :])
    rows = jnp.concatenate(rows + [jnp.zeros((5, 128), f32)], axis=0)
    near = dot(rows.astype(bf16), spread).astype(jnp.int32)
    source = iota((5 * COL, COL), 0)
    sums = []
    for o in range(3):
        own = source == lane + (o + 1) * COL
        total = jnp.where(own, 1.0 - 0.5 * edges, 0.0)
        for s in range(4):
            element = near[o : o + 1, s * COL : (s + 1) * COL]
            relative = lax.rem(element // 4 - device + (2 + SPANS), SPANS)
            target = relative * COL + facing[s] * 4 + element % 4
            target = jnp.where(on_edge[s], target, -1)
            total = total + jnp.where(source == target, 0.5, 0.0)
        sums.append(total)
    second = dot(sums[1][COL : 4 * COL].astype(bf16), lap).astype(bf16)
    matrix = jnp.zeros((5 * COL, COL), f32)
    for o in range(3):
        inner = dot(lap, second[o * COL : (o + 1) * COL]).astype(bf16)
        matrix = matrix + dot(sums[o].astype(bf16), inner)
    matrix = sums[1] - viscosity * matrix
    zero = jnp.zeros((COL, COL), f32)
    for o in range(5):
        block = matrix[o * COL : (o + 1) * COL]
        matrix_ref[o] = jnp.concatenate(
            [jnp.concatenate([block, zero], axis=1), jnp.concatenate([zero, block], axis=1)], axis=0
        )


def span_kernel(
    recv_ref, diff_ref, courant_ref, cloud_ref, lap_ref, out_ref, matrix_ref,
    state_ref, rate_ref, part_ref, ratio_ref,
):
    halo_matrix(recv_ref, lap_ref, matrix_ref)
    rate_ref[...] = active_rate(courant_ref[...], cloud_ref[...])
    for k in range(CHUNKS - 1):
        state_ref[pl.ds(128 * k, 128), :] = chunk_t(recv_ref, k)
    groups = [strided(state_ref, out_ref, g * PAIR * LEV) for g in range(2)]
    solve(diff_ref, rate_ref, groups, part_ref, ratio_ref)


def dynamics_kernel(a_ref, b_ref, c_ref, d_ref, e_ref, matrix_ref, out_ref):
    total = jnp.zeros((PAIR * LEV, 128), f32)
    for o, ref in enumerate((a_ref, b_ref, c_ref, d_ref, e_ref)):
        x_hi, x_lo = split2(ref[...])
        m_hi, m_lo = split2(matrix_ref[o])
        total = total + (dot(x_hi, m_hi) + dot(x_lo, m_hi) + dot(x_hi, m_lo))
    for f in range(PAIR):
        turned = total[f * LEV : (f + 1) * LEV].T
        out_ref[f] = turned[:COL]
        out_ref[f + PAIR] = turned[COL:]


def per_device(column_state, span_of, diffusivity, courant, cloud_levels, neighbors):
    shape = jax.ShapeDtypeStruct
    params = pltpu.CompilerParams(vmem_limit_bytes=32 * 1024 * 1024)
    x = jnp.transpose(column_state, (1, 2, 0))
    span_row = span_of.reshape(1, COL)
    cloud_row = cloud_levels.reshape(1, SLOT)
    message, slots = pl.pallas_call(
        pack_kernel,
        out_shape=(shape((SLOT * CHUNKS, 128), f32), shape((8, SLOT), jnp.int32)),
        compiler_params=params,
        name="pack",
    )(x, span_row, diffusivity, courant, cloud_row, neighbors)
    turned = pl.pallas_call(
        turn_kernel,
        out_shape=shape((PAIR * LEV, 128), f32),
        compiler_params=params,
        name="turn",
    )(x)
    received = lax.all_to_all(
        message.reshape(SPANS, 16, 128), "curve", split_axis=0, concat_axis=0, tiled=True
    ).reshape(SLOT * CHUNKS, 128)
    physics = pl.pallas_call(
        element_kernel,
        out_shape=shape((PAIR * LEV, 128), f32),
        scratch_shapes=[
            pltpu.VMEM((LEV, 128), f32),
            pltpu.VMEM((LEV, 128), f32),
            pltpu.VMEM((1, LEV, PAIR, 128), f32),
            pltpu.VMEM((LEV, PAIR, 128), f32),
        ],
        compiler_params=params,
        name="element",
    )(received, slots, turned)
    halo = {}
    for k in (2, 1, -1, -2):
        halo[k] = lax.ppermute(physics, "curve", [(i, (i + k) % SPANS) for i in range(SPANS)])
    span_state, matrix = pl.pallas_call(
        span_kernel,
        out_shape=(shape((STATE, SLOT), f32), shape((5, 128, 128), f32)),
        scratch_shapes=[
            pltpu.VMEM(((CHUNKS - 1) * 128, 128), f32),
            pltpu.VMEM((LEV, 128), f32),
            pltpu.VMEM((2, LEV, PAIR, 128), f32),
            pltpu.VMEM((LEV, PAIR, 128), f32),
        ],
        compiler_params=params,
        name="span",
    )(received, diffusivity, courant, cloud_row, jnp.asarray(lap_columns))
    dynamics = pl.pallas_call(
        dynamics_kernel,
        out_shape=shape((NF, COL, LEV), f32),
        compiler_params=params,
        name="dynamics",
    )(halo[2], halo[1], physics, halo[-1], halo[-2], matrix)
    return (
        jnp.transpose(span_state.reshape(NF, LEV, SLOT), (1, 0, 2)),
        jnp.transpose(dynamics, (2, 0, 1)),
    )


def solution(mesh):
    placed = (
        P(None, "field", "curve"),
        P("curve"),
        P(None, "curve"),
        P(None, "curve"),
        P("curve"),
        P(None, "curve"),
    )
    return jax.shard_map(
        per_device,
        mesh=mesh,
        in_specs=placed,
        out_specs=(P(None, "field", "curve"), P(None, "field", "curve")),
        check_vma=False,
    )
```

```python
import numpy as np
import jax
import jax.numpy as jnp
from jax import lax
from jax.experimental import pallas as pl
from jax.experimental.pallas import tpu as pltpu
from jax.sharding import PartitionSpec as P

LEV = 72
HALF = LEV // 2
NF = 12
PAIR = NF // 2
COL = 64
SLOT = 128
WORDS = 1024
CHUNKS = WORDS // 128
STATE = NF * LEV
SPANS = 64
viscosity = 0.02

second_diff = np.array(
    [[-1.0, 1.0, 0.0, 0.0], [1.0, -2.0, 1.0, 0.0], [0.0, 1.0, -2.0, 1.0], [0.0, 0.0, 1.0, -1.0]]
)
lap_nodes = np.kron(np.eye(4), second_diff) + np.kron(second_diff, np.eye(4))
lap_columns = np.kron(lap_nodes, np.eye(4)).astype(np.float32)

f32 = jnp.float32
bf16 = jnp.bfloat16


def iota(shape, axis):
    return lax.broadcasted_iota(jnp.int32, shape, axis)


def split3(x):
    hi = x.astype(bf16)
    rest = x - hi.astype(f32)
    mid = rest.astype(bf16)
    lo = (rest - mid.astype(f32)).astype(bf16)
    return hi, mid, lo


def split2(x):
    hi = x.astype(bf16)
    return hi, (x - hi.astype(f32)).astype(bf16)


def dot(a, b):
    return jnp.dot(a, b, preferred_element_type=f32)


def slots_of(span_row):
    row = span_row.astype(f32)
    square = jnp.broadcast_to(row, (COL, COL))
    column = jnp.sum(
        jnp.where(iota((COL, COL), 0) == iota((COL, COL), 1), square, 0.0), axis=1, keepdims=True
    )
    earlier = jnp.logical_and(column == square, iota((COL, COL), 0) < iota((COL, COL), 1))
    rank = jnp.sum(jnp.where(earlier, 1.0, 0.0), axis=0, keepdims=True)
    return (2.0 * row + rank).astype(jnp.int32)


def active_rate(courant, cloud_row):
    level = iota((LEV, SLOT), 0)
    return jnp.where(level >= LEV - cloud_row, courant, 0.0)


def fetch(sources, targets, sems):
    copies = [
        pltpu.make_async_copy(source, target, sems.at[i])
        for i, (source, target) in enumerate(zip(sources, targets))
    ]
    for copy in copies:
        copy.start()
    return copies


def pack_kernel(
    x_hbm, span_hbm, diff_hbm, courant_hbm, cloud_hbm, near_hbm, out_ref, slot_ref,
    x_ref, span_ref, diff_ref, courant_ref, cloud_ref, near_ref, sems,
):
    copies = fetch(
        (span_hbm, cloud_hbm, near_hbm, diff_hbm, courant_hbm, x_hbm),
        (span_ref, cloud_ref, near_ref, diff_ref, courant_ref, x_ref),
        sems,
    )
    for copy in copies[:5]:
        copy.wait()
    slot_row = slots_of(span_ref[...])
    slot_ref[...] = jnp.broadcast_to(jnp.concatenate([slot_row, slot_row], axis=1), (8, SLOT))
    pick = (iota((SLOT, COL), 0) == slot_row).astype(f32).astype(bf16)
    diff_t = diff_ref[...].T
    rate_t = active_rate(courant_ref[...], cloud_ref[...]).T
    near = near_ref[...].astype(f32)
    near_row = jnp.concatenate([near[s : s + 1, :] for s in range(4)], axis=1)
    near_t = jnp.broadcast_to(near_row, (SLOT, 16))
    copies[5].wait()
    state = jnp.concatenate([x_ref[f] for f in range(NF)], axis=1)
    hi, mid, lo = split3(state)
    packed = dot(pick, hi) + dot(pick, mid) + dot(pick, lo)
    message = jnp.concatenate([packed, diff_t, rate_t, near_t], axis=1)
    for k in range(CHUNKS):
        out_ref[pl.ds(k, SLOT, stride=CHUNKS), :] = message[:, 128 * k : 128 * k + 128]


def turn_kernel(x_hbm, out_ref, x_ref, sems):
    fetch((x_hbm,), (x_ref,), sems)[0].wait()
    for f in range(PAIR):
        both = jnp.concatenate([x_ref[f], x_ref[f + PAIR]], axis=0)
        out_ref[pl.ds(f * LEV, LEV), :] = both.T


def chunk_t(recv_ref, k):
    return recv_ref[pl.ds(k, SLOT, stride=CHUNKS), :].T


def solve(coef_ref, rate_ref, groups, part_ref, ratio_ref):
    rows = (PAIR, 128)
    zero = jnp.zeros(rows, f32)

    def row(ref, k):
        return jnp.broadcast_to(ref[pl.ds(k, 1), :], rows)

    count = len(groups)
    top_ratio, bot_ratio = zero, zero
    top_part, bot_part = [zero] * count, [zero] * count
    top_flux = [zero] * count
    top_above = zero
    bot_below = row(coef_ref, LEV - 1)
    last = row(rate_ref, LEV - 1)
    bot_state = [load(LEV - 1) for load, _ in groups]
    bot_flux = [last * x for x in bot_state]
    for i in range(HALF):
        t, u = i, LEV - 1 - i
        top_next = row(coef_ref, t)
        bot_next = row(coef_ref, u - 1)
        top_inv = 1.0 / (1.0 + top_above + top_next - top_above * top_ratio)
        bot_inv = 1.0 / (1.0 + bot_below + bot_next - bot_below * bot_ratio)
        top_ratio = top_next * top_inv
        bot_ratio = bot_next * bot_inv
        ratio_ref[i] = top_ratio
        ratio_ref[HALF + i] = bot_ratio
        top_rate = row(rate_ref, t)
        above_rate = row(rate_ref, u - 1)
        for g, (load, _) in enumerate(groups):
            x = load(t)
            flux = top_rate * x
            settled = x - flux + top_flux[g]
            top_flux[g] = flux
            top_part[g] = (settled + top_above * top_part[g]) * top_inv
            part_ref[g, i] = top_part[g]
            above = load(u - 1)
            above_flux = above_rate * above
            settled = bot_state[g] - bot_flux[g] + above_flux
            bot_state[g] = above
            bot_flux[g] = above_flux
            bot_part[g] = (settled + bot_below * bot_part[g]) * bot_inv
            part_ref[g, HALF + i] = bot_part[g]
        top_above = top_next
        bot_below = bot_next
    meet = 1.0 / (1.0 - top_ratio * bot_ratio)
    top, bot = [], []
    for g, (_, store) in enumerate(groups):
        top.append((top_part[g] + top_ratio * bot_part[g]) * meet)
        bot.append((bot_part[g] + bot_ratio * top_part[g]) * meet)
        store(HALF - 1, top[g])
        store(HALF, bot[g])
    for i in range(HALF - 2, -1, -1):
        top_ratio = ratio_ref[i]
        bot_ratio = ratio_ref[HALF + i]
        for g, (_, store) in enumerate(groups):
            top[g] = part_ref[g, i] + top_ratio * top[g]
            bot[g] = part_ref[g, HALF + i] + bot_ratio * bot[g]
            store(i, top[g])
            store(LEV - 1 - i, bot[g])


def strided(in_ref, out_ref, base):
    def load(level):
        return in_ref[pl.ds(base + level, PAIR, stride=LEV), :]

    def store(level, value):
        out_ref[pl.ds(base + level, PAIR, stride=LEV), :] = value

    return load, store


def element_kernel(recv_ref, slot_ref, x_ref, out_ref, coef_ref, rate_ref, part_ref, ratio_ref):
    spread = (iota((SLOT, 128), 0) == slot_ref[0:1, :]).astype(f32).astype(bf16)
    tail = jnp.concatenate([chunk_t(recv_ref, CHUNKS - 2), chunk_t(recv_ref, CHUNKS - 1)], axis=0)
    begin = STATE - 128 * (CHUNKS - 2)
    hi, mid, lo = split3(tail[begin : begin + 2 * LEV])
    columns = dot(hi, spread) + dot(mid, spread) + dot(lo, spread)
    coef_ref[...] = columns[:LEV]
    rate_ref[...] = columns[LEV:]
    solve(coef_ref, rate_ref, [strided(x_ref, out_ref, 0)], part_ref, ratio_ref)


def halo_matrix(recv_ref, lap_ref, matrix_ref):
    device = lax.axis_index("curve")
    lap = lap_ref[...].astype(bf16)
    lane = iota((1, COL), 1)
    node = lane // 4
    node_row, node_col = node // 4, node % 4
    on_edge = [node_row == 0, node_col == 3, node_row == 3, node_col == 0]
    facing = [node + 12, node - 3, node - 12, node + 3]
    edges = sum(jnp.where(edge, 1.0, 0.0) for edge in on_edge)
    word = iota((128, 4 * COL), 0) - (128 - 16)
    place = iota((128, 4 * COL), 1)
    spread = (word == (place // COL) * 4 + place % 4).astype(f32).astype(bf16)
    rows = []
    for o in range(3):
        block = lax.rem(device + (o - 1) + SPANS, SPANS)
        rows.append(recv_ref[pl.ds(block * 16 + CHUNKS - 1, 1), :])
    rows = jnp.concatenate(rows + [jnp.zeros((5, 128), f32)], axis=0)
    near = dot(rows.astype(bf16), spread).astype(jnp.int32)
    source = iota((5 * COL, COL), 0)
    sums = []
    for o in range(3):
        own = source == lane + (o + 1) * COL
        total = jnp.where(own, 1.0 - 0.5 * edges, 0.0)
        for s in range(4):
            element = near[o : o + 1, s * COL : (s + 1) * COL]
            relative = lax.rem(element // 4 - device + (2 + SPANS), SPANS)
            target = relative * COL + facing[s] * 4 + element % 4
            target = jnp.where(on_edge[s], target, -1)
            total = total + jnp.where(source == target, 0.5, 0.0)
        sums.append(total)
    second = dot(sums[1][COL : 4 * COL].astype(bf16), lap).astype(bf16)
    matrix = jnp.zeros((5 * COL, COL), f32)
    for o in range(3):
        inner = dot(lap, second[o * COL : (o + 1) * COL]).astype(bf16)
        matrix = matrix + dot(sums[o].astype(bf16), inner)
    matrix = sums[1] - viscosity * matrix
    zero = jnp.zeros((COL, COL), bf16)
    for place, o in enumerate((2, 1, 3, 0, 4)):
        halves = []
        for block in split2(matrix[o * COL : (o + 1) * COL]):
            top = jnp.concatenate([block, zero], axis=1)
            bottom = jnp.concatenate([zero, block], axis=1)
            halves.append(jnp.concatenate([top, bottom], axis=0))
        matrix_ref[pl.ds(place * 128, 128), :] = jnp.concatenate(halves, axis=1)


def apply(x, matrix):
    hi, lo = split2(x)
    both = dot(hi, matrix)
    return both[:, :128] + both[:, 128:] + dot(lo, matrix[:, :128])


def span_kernel(
    recv_ref, diff_ref, courant_ref, cloud_ref, lap_ref, own_ref, out_ref, matrix_ref, part_sum_ref,
    state_ref, rate_ref, part_ref, ratio_ref,
):
    halo_matrix(recv_ref, lap_ref, matrix_ref)
    rate_ref[...] = active_rate(courant_ref[...], cloud_ref[...])
    for k in range(CHUNKS - 1):
        state_ref[pl.ds(128 * k, 128), :] = chunk_t(recv_ref, k)
    groups = [strided(state_ref, out_ref, g * PAIR * LEV) for g in range(2)]
    solve(diff_ref, rate_ref, groups, part_ref, ratio_ref)
    part_sum_ref[...] = apply(own_ref[...], matrix_ref[pl.ds(0, 128), :])


def beside_kernel(below_ref, above_ref, part_ref, matrix_ref, out_ref):
    x = jnp.concatenate([below_ref[...], above_ref[...]], axis=1)
    out_ref[...] = part_ref[...] + apply(x, matrix_ref[pl.ds(128, 256), :])


def beyond_kernel(below_ref, above_ref, part_ref, matrix_ref, out_hbm, out_ref, sems):
    x = jnp.concatenate([below_ref[...], above_ref[...]], axis=1)
    total = part_ref[...] + apply(x, matrix_ref[pl.ds(384, 256), :])
    copies = []
    for f in range(PAIR):
        turned = total[f * LEV : (f + 1) * LEV].T
        out_ref[f] = turned[:COL]
        out_ref[f + PAIR] = turned[COL:]
        for at in (f, f + PAIR):
            copy = pltpu.make_async_copy(out_ref.at[at], out_hbm.at[at], sems.at[at])
            copy.start()
            copies.append(copy)
    for copy in copies:
        copy.wait()


def in_hbm(array):
    return pltpu.with_memory_space_constraint(array, pltpu.HBM)


def per_device(column_state, span_of, diffusivity, courant, cloud_levels, neighbors):
    shape = jax.ShapeDtypeStruct
    params = pltpu.CompilerParams(vmem_limit_bytes=32 * 1024 * 1024)
    x = jnp.transpose(column_state, (1, 2, 0))
    span_row = span_of.reshape(1, COL)
    cloud_row = cloud_levels.reshape(1, SLOT)
    hbm = pl.BlockSpec(memory_space=pltpu.HBM)
    message, slots = pl.pallas_call(
        pack_kernel,
        out_shape=(shape((SLOT * CHUNKS, 128), f32), shape((8, SLOT), jnp.int32)),
        in_specs=[hbm] * 6,
        scratch_shapes=[
            pltpu.VMEM((NF, COL, LEV), f32),
            pltpu.VMEM((1, COL), jnp.int32),
            pltpu.VMEM((LEV, SLOT), f32),
            pltpu.VMEM((LEV, SLOT), f32),
            pltpu.VMEM((1, SLOT), jnp.int32),
            pltpu.VMEM((4, 4), jnp.int32),
            pltpu.SemaphoreType.DMA((6,)),
        ],
        compiler_params=params,
        name="pack",
    )(*(in_hbm(a) for a in (x, span_row, diffusivity, courant, cloud_row, neighbors)))
    turned = pl.pallas_call(
        turn_kernel,
        out_shape=shape((PAIR * LEV, 128), f32),
        in_specs=[hbm],
        scratch_shapes=[pltpu.VMEM((NF, COL, LEV), f32), pltpu.SemaphoreType.DMA((1,))],
        compiler_params=params,
        name="turn",
    )(in_hbm(x))
    received = lax.all_to_all(
        message.reshape(SPANS, 16, 128), "curve", split_axis=0, concat_axis=0, tiled=True
    ).reshape(SLOT * CHUNKS, 128)
    physics = pl.pallas_call(
        element_kernel,
        out_shape=shape((PAIR * LEV, 128), f32),
        scratch_shapes=[
            pltpu.VMEM((LEV, 128), f32),
            pltpu.VMEM((LEV, 128), f32),
            pltpu.VMEM((1, LEV, PAIR, 128), f32),
            pltpu.VMEM((LEV, PAIR, 128), f32),
        ],
        compiler_params=params,
        name="element",
    )(received, slots, turned)
    halo = {}
    for k in (1, -1, 2, -2):
        halo[k] = lax.ppermute(physics, "curve", [(i, (i + k) % SPANS) for i in range(SPANS)])
    span_state, matrix, total = pl.pallas_call(
        span_kernel,
        out_shape=(
            shape((STATE, SLOT), f32), shape((640, 256), bf16), shape((PAIR * LEV, 128), f32)
        ),
        scratch_shapes=[
            pltpu.VMEM(((CHUNKS - 1) * 128, 128), f32),
            pltpu.VMEM((LEV, 128), f32),
            pltpu.VMEM((2, LEV, PAIR, 128), f32),
            pltpu.VMEM((LEV, PAIR, 128), f32),
        ],
        compiler_params=params,
        name="span",
    )(received, diffusivity, courant, cloud_row, jnp.asarray(lap_columns), physics)
    total = pl.pallas_call(
        beside_kernel,
        out_shape=shape((PAIR * LEV, 128), f32),
        compiler_params=params,
        name="beside",
    )(halo[1], halo[-1], total, matrix)
    dynamics = pl.pallas_call(
        beyond_kernel,
        out_shape=shape((NF, COL, LEV), f32),
        out_specs=hbm,
        scratch_shapes=[pltpu.VMEM((NF, COL, LEV), f32), pltpu.SemaphoreType.DMA((NF,))],
        compiler_params=params,
        name="beyond",
    )(halo[2], halo[-2], total, matrix)
    return (
        jnp.transpose(span_state.reshape(NF, LEV, SLOT), (1, 0, 2)),
        jnp.transpose(dynamics, (2, 0, 1)),
    )


def solution(mesh):
    placed = (
        P(None, "field", "curve"),
        P("curve"),
        P(None, "curve"),
        P(None, "curve"),
        P("curve"),
        P(None, "curve"),
    )
    return jax.shard_map(
        per_device,
        mesh=mesh,
        in_specs=placed,
        out_specs=(P(None, "field", "curve"), P(None, "field", "curve")),
        check_vma=False,
    )
```

```python
import numpy as np
import jax
import jax.numpy as jnp
from jax import lax
from jax.experimental import pallas as pl
from jax.experimental.pallas import tpu as pltpu
from jax.sharding import PartitionSpec as P

LEV = 72
HALF = LEV // 2
NF = 12
PAIR = NF // 2
COL = 64
SLOT = 128
WORDS = 1024
CHUNKS = WORDS // 128
STATE = NF * LEV
SPANS = 64
viscosity = 0.02

second_diff = np.array(
    [[-1.0, 1.0, 0.0, 0.0], [1.0, -2.0, 1.0, 0.0], [0.0, 1.0, -2.0, 1.0], [0.0, 0.0, 1.0, -1.0]]
)
lap_nodes = np.kron(np.eye(4), second_diff) + np.kron(second_diff, np.eye(4))
lap_columns = np.kron(lap_nodes, np.eye(4)).astype(np.float32)

f32 = jnp.float32
bf16 = jnp.bfloat16


def iota(shape, axis):
    return lax.broadcasted_iota(jnp.int32, shape, axis)


def split3(x):
    hi = x.astype(bf16)
    rest = x - hi.astype(f32)
    mid = rest.astype(bf16)
    lo = (rest - mid.astype(f32)).astype(bf16)
    return hi, mid, lo


def split2(x):
    hi = x.astype(bf16)
    return hi, (x - hi.astype(f32)).astype(bf16)


def dot(a, b):
    return jnp.dot(a, b, preferred_element_type=f32)


def slots_of(span_row):
    row = span_row.astype(f32)
    square = jnp.broadcast_to(row, (COL, COL))
    column = jnp.sum(
        jnp.where(iota((COL, COL), 0) == iota((COL, COL), 1), square, 0.0), axis=1, keepdims=True
    )
    earlier = jnp.logical_and(column == square, iota((COL, COL), 0) < iota((COL, COL), 1))
    rank = jnp.sum(jnp.where(earlier, 1.0, 0.0), axis=0, keepdims=True)
    return (2.0 * row + rank).astype(jnp.int32)


def active_rate(courant, cloud_row):
    level = iota((LEV, SLOT), 0)
    return jnp.where(level >= LEV - cloud_row, courant, 0.0)


def fetch(sources, targets, sems):
    copies = [
        pltpu.make_async_copy(source, target, sems.at[i])
        for i, (source, target) in enumerate(zip(sources, targets))
    ]
    for copy in copies:
        copy.start()
    return copies


def pack_kernel(
    x_hbm, span_hbm, diff_hbm, courant_hbm, cloud_hbm, near_hbm, out_ref, slot_ref,
    x_ref, span_ref, diff_ref, courant_ref, cloud_ref, near_ref, sems,
):
    copies = fetch(
        (span_hbm, cloud_hbm, near_hbm, diff_hbm, courant_hbm, x_hbm),
        (span_ref, cloud_ref, near_ref, diff_ref, courant_ref, x_ref),
        sems,
    )
    for copy in copies[:5]:
        copy.wait()
    slot_row = slots_of(span_ref[...])
    slot_ref[...] = jnp.broadcast_to(jnp.concatenate([slot_row, slot_row], axis=1), (8, SLOT))
    pick = (iota((SLOT, COL), 0) == slot_row).astype(f32).astype(bf16)
    diff_t = diff_ref[...].T
    rate_t = active_rate(courant_ref[...], cloud_ref[...]).T
    near = near_ref[...].astype(f32)
    near_row = jnp.concatenate([near[s : s + 1, :] for s in range(4)], axis=1)
    near_t = jnp.broadcast_to(near_row, (SLOT, 16))
    copies[5].wait()
    state = jnp.concatenate([x_ref[f] for f in range(NF)], axis=1)
    hi, mid, lo = split3(state)
    packed = dot(pick, hi) + dot(pick, mid) + dot(pick, lo)
    message = jnp.concatenate([packed, diff_t, rate_t, near_t], axis=1)
    for k in range(CHUNKS):
        out_ref[pl.ds(k, SLOT, stride=CHUNKS), :] = message[:, 128 * k : 128 * k + 128]


def turn_kernel(x_hbm, out_ref, x_ref, sems):
    fetch((x_hbm,), (x_ref,), sems)[0].wait()
    for f in range(PAIR):
        both = jnp.concatenate([x_ref[f], x_ref[f + PAIR]], axis=0)
        out_ref[pl.ds(f * LEV, LEV), :] = both.T


def chunk_t(recv_ref, k):
    return recv_ref[pl.ds(k, SLOT, stride=CHUNKS), :].T


def solve(coef_ref, rate_ref, groups, part_ref, ratio_ref):
    rows = (PAIR, 128)
    zero = jnp.zeros(rows, f32)

    def row(ref, k):
        return jnp.broadcast_to(ref[pl.ds(k, 1), :], rows)

    count = len(groups)
    top_ratio, bot_ratio = zero, zero
    top_part, bot_part = [zero] * count, [zero] * count
    top_flux = [zero] * count
    top_above = zero
    bot_below = row(coef_ref, LEV - 1)
    last = row(rate_ref, LEV - 1)
    bot_state = [load(LEV - 1) for load, _ in groups]
    bot_flux = [last * x for x in bot_state]
    for i in range(HALF):
        t, u = i, LEV - 1 - i
        top_next = row(coef_ref, t)
        bot_next = row(coef_ref, u - 1)
        top_inv = 1.0 / (1.0 + top_above + top_next - top_above * top_ratio)
        bot_inv = 1.0 / (1.0 + bot_below + bot_next - bot_below * bot_ratio)
        top_ratio = top_next * top_inv
        bot_ratio = bot_next * bot_inv
        ratio_ref[i] = top_ratio
        ratio_ref[HALF + i] = bot_ratio
        top_rate = row(rate_ref, t)
        above_rate = row(rate_ref, u - 1)
        for g, (load, _) in enumerate(groups):
            x = load(t)
            flux = top_rate * x
            settled = x - flux + top_flux[g]
            top_flux[g] = flux
            top_part[g] = (settled + top_above * top_part[g]) * top_inv
            part_ref[g, i] = top_part[g]
            above = load(u - 1)
            above_flux = above_rate * above
            settled = bot_state[g] - bot_flux[g] + above_flux
            bot_state[g] = above
            bot_flux[g] = above_flux
            bot_part[g] = (settled + bot_below * bot_part[g]) * bot_inv
            part_ref[g, HALF + i] = bot_part[g]
        top_above = top_next
        bot_below = bot_next
    meet = 1.0 / (1.0 - top_ratio * bot_ratio)
    top, bot = [], []
    for g, (_, store) in enumerate(groups):
        top.append((top_part[g] + top_ratio * bot_part[g]) * meet)
        bot.append((bot_part[g] + bot_ratio * top_part[g]) * meet)
        store(HALF - 1, top[g])
        store(HALF, bot[g])
    for i in range(HALF - 2, -1, -1):
        top_ratio = ratio_ref[i]
        bot_ratio = ratio_ref[HALF + i]
        for g, (_, store) in enumerate(groups):
            top[g] = part_ref[g, i] + top_ratio * top[g]
            bot[g] = part_ref[g, HALF + i] + bot_ratio * bot[g]
            store(i, top[g])
            store(LEV - 1 - i, bot[g])


def strided(in_ref, out_ref, base):
    def load(level):
        return in_ref[pl.ds(base + level, PAIR, stride=LEV), :]

    def store(level, value):
        out_ref[pl.ds(base + level, PAIR, stride=LEV), :] = value

    return load, store


def element_kernel(
    recv_ref, slot_ref, x_ref, out_ref, near_ref, far_ref, coef_ref, rate_ref, part_ref, ratio_ref
):
    device = lax.axis_index("curve")
    spread = (iota((SLOT, 128), 0) == slot_ref[0:1, :]).astype(f32).astype(bf16)
    tail = jnp.concatenate([chunk_t(recv_ref, CHUNKS - 2), chunk_t(recv_ref, CHUNKS - 1)], axis=0)
    begin = STATE - 128 * (CHUNKS - 2)
    hi, mid, lo = split3(tail[begin : begin + 2 * LEV])
    columns = dot(hi, spread) + dot(mid, spread) + dot(lo, spread)
    coef_ref[...] = columns[:LEV]
    rate_ref[...] = columns[LEV:]
    element, relative = neighbour_lanes(recv_ref, device)
    cuts = []
    for o, beyond in ((2, 4), (0, 0)):
        reach = jnp.zeros((COL, COL), f32)
        for s in range(4):
            reach = reach + edge_entries(element, relative, o, s, COL, 2)
        flags = [relative[o][s][:, :32] == beyond for s in range(4)]
        cuts.append(dot(reach.astype(bf16), corner_choice(flags).astype(bf16)))
    up, down = cuts
    odd = lax.rem(device // 2, 2) == 1
    first, second = jnp.where(odd, down, up), jnp.where(odd, up, down)
    zero = jnp.zeros((COL, 32), f32)
    matrix = jnp.concatenate(
        [
            jnp.concatenate([first, zero, second, zero], axis=1),
            jnp.concatenate([zero, first, zero, second], axis=1),
        ],
        axis=0,
    ).astype(bf16)
    solve(coef_ref, rate_ref, [strided(x_ref, out_ref, 0)], part_ref, ratio_ref)
    hi, lo = split2(out_ref[...])
    cut = dot(hi, matrix) + dot(lo, matrix)
    half = PAIR * LEV // 2
    near_ref[...] = jnp.concatenate([cut[:half, :COL], cut[half:, :COL]], axis=1)
    far_ref[...] = jnp.concatenate([cut[:half, COL:], cut[half:, COL:]], axis=1)


def edge_places():
    lane = iota((1, COL), 1)
    node = lane // 4
    node_row, node_col = node // 4, node % 4
    on_edge = [node_row == 0, node_col == 3, node_row == 3, node_col == 0]
    facing = [node + 12, node - 3, node - 12, node + 3]
    return lane, on_edge, facing


def neighbour_lanes(recv_ref, device):
    word = iota((128, 4 * COL), 0) - (128 - 16)
    place = iota((128, 4 * COL), 1)
    spread = (word == (place // COL) * 4 + place % 4).astype(f32).astype(bf16)
    rows = []
    for o in range(3):
        block = lax.rem(device + (o - 1) + SPANS, SPANS)
        rows.append(recv_ref[pl.ds(block * 16 + CHUNKS - 1, 1), :])
    rows = jnp.concatenate(rows + [jnp.zeros((5, 128), f32)], axis=0)
    near = dot(rows.astype(bf16), spread).astype(jnp.int32)
    far = lax.rem(near // 4 - device + (2 + SPANS), SPANS)
    cut = [slice(s * COL, (s + 1) * COL) for s in range(4)]
    element = [[near[o : o + 1, c] % 4 for c in cut] for o in range(3)]
    relative = [[far[o : o + 1, c] for c in cut] for o in range(3)]
    return element, relative


def edge_entries(element, relative, o, s, rows, only=None):
    lane, on_edge, facing = edge_places()
    target = facing[s] * 4 + element[o][s]
    keep = on_edge[s]
    if only is None:
        target = target + relative[o][s] * COL
    else:
        keep = jnp.logical_and(keep, relative[o][s] == only)
    target = jnp.where(keep, target, -1)
    return jnp.where(iota((rows, COL), 0) == target, 0.5, 0.0)


def corner_choice(flags):
    lane = iota((1, 32), 1)
    j = (lane % 16) // 4
    up, right = j // 2, j % 2
    on_row = jnp.where(up == 0, flags[0].astype(f32), flags[2].astype(f32))
    on_col = jnp.where(right == 0, flags[3].astype(f32), flags[1].astype(f32))
    place = iota((COL, 32), 0)
    same = place % 4 == lane % 4
    node = place // 4
    corner = jnp.where(node == up * 12 + right * 3, 1.0, 0.0)
    side = jnp.where(node == (1 + up) * 4 + right * 3, on_row, 0.0)
    side = side + jnp.where(node == up * 12 + 1 + right, on_col, 0.0)
    return jnp.where(same, jnp.where(lane < 16, corner, side), 0.0)


def twice(block):
    zero = jnp.zeros(block.shape, block.dtype)
    top = jnp.concatenate([block, zero], axis=1)
    return jnp.concatenate([top, jnp.concatenate([zero, block], axis=1)], axis=0)


def halo_matrix(recv_ref, lap_ref, matrix_ref, cut_ref):
    device = lax.axis_index("curve")
    lap = lap_ref[...].astype(bf16)
    element, relative = neighbour_lanes(recv_ref, device)
    lane, on_edge, _ = edge_places()
    edges = sum(jnp.where(edge, 1.0, 0.0) for edge in on_edge)
    source = iota((5 * COL, COL), 0)
    sums = []
    for o in range(3):
        own = source == lane + (o + 1) * COL
        total = jnp.where(own, 1.0 - 0.5 * edges, 0.0)
        for s in range(4):
            total = total + edge_entries(element, relative, o, s, 5 * COL)
        sums.append(total)
    second = dot(sums[1][COL : 4 * COL].astype(bf16), lap).astype(bf16)
    matrix = jnp.zeros((3 * COL, COL), f32)
    inner = []
    for o in range(3):
        inner.append(dot(lap, second[o * COL : (o + 1) * COL]).astype(bf16))
        matrix = matrix + dot(sums[o][COL : 4 * COL].astype(bf16), inner[o])
    matrix = sums[1][COL : 4 * COL] - viscosity * matrix
    core = lax.rem(device, 2)
    for o, place in ((0, 1 + core), (1, 0), (2, 2 - core)):
        halves = [twice(block) for block in split2(matrix[o * COL : (o + 1) * COL])]
        start = pl.multiple_of(place * 128, 128)
        matrix_ref[pl.ds(start, 128), :] = jnp.concatenate(halves, axis=1)
    parts = []
    for o in (0, 2):
        flags = [relative[o][s][:, :32] == 2 for s in range(4)]
        choice = corner_choice(flags).astype(bf16)
        parts.append(
            -viscosity
            * lax.dot_general(
                choice, inner[o], (((0,), (0,)), ((), ())), preferred_element_type=f32
            )
        )
    down, up = parts
    odd = lax.rem(device // 2, 2) == 1
    far, near = jnp.where(odd, up, down), jnp.where(odd, down, up)
    for i, block in enumerate((far, near)):
        for h, half in enumerate(split2(block)):
            cut_ref[h, pl.ds(i * 128, 128), :] = twice(twice(half))


def apply(x, matrix):
    hi, lo = split2(x)
    both = dot(hi, matrix)
    return both[:, :128] + both[:, 128:] + dot(lo, matrix[:, :128])


def span_kernel(
    recv_ref, diff_ref, courant_ref, cloud_ref, lap_ref, own_ref,
    out_ref, matrix_ref, cut_ref, part_sum_ref,
    state_ref, rate_ref, part_ref, ratio_ref,
):
    halo_matrix(recv_ref, lap_ref, matrix_ref, cut_ref)
    rate_ref[...] = active_rate(courant_ref[...], cloud_ref[...])
    for k in range(CHUNKS - 1):
        state_ref[pl.ds(128 * k, 128), :] = chunk_t(recv_ref, k)
    groups = [strided(state_ref, out_ref, g * PAIR * LEV) for g in range(2)]
    solve(diff_ref, rate_ref, groups, part_ref, ratio_ref)
    part_sum_ref[...] = apply(own_ref[...], matrix_ref[pl.ds(0, 128), :])


def beside_kernel(across_ref, chip_ref, part_ref, matrix_ref, out_ref):
    x = jnp.concatenate([across_ref[...], chip_ref[...]], axis=1)
    out_ref[...] = part_ref[...] + apply(x, matrix_ref[pl.ds(128, 256), :])


def beyond_kernel(far_ref, near_ref, part_ref, cut_ref, out_hbm, out_ref, sems):
    hi, lo = split2(jnp.concatenate([far_ref[...], near_ref[...]], axis=1))
    cut = dot(hi, cut_ref[0]) + dot(lo, cut_ref[0]) + dot(hi, cut_ref[1])
    total = part_ref[...] + jnp.concatenate([cut[:, :128], cut[:, 128:]], axis=0)
    copies = []
    for f in range(PAIR):
        turned = total[f * LEV : (f + 1) * LEV].T
        out_ref[f] = turned[:COL]
        out_ref[f + PAIR] = turned[COL:]
        for at in (f, f + PAIR):
            copy = pltpu.make_async_copy(out_ref.at[at], out_hbm.at[at], sems.at[at])
            copy.start()
            copies.append(copy)
    for copy in copies:
        copy.wait()


def swap(x, partner):
    return lax.ppermute(x, "curve", [(i, partner(i) % SPANS) for i in range(SPANS)])


def in_hbm(array):
    return pltpu.with_memory_space_constraint(array, pltpu.HBM)


def per_device(column_state, span_of, diffusivity, courant, cloud_levels, neighbors):
    shape = jax.ShapeDtypeStruct
    params = pltpu.CompilerParams(vmem_limit_bytes=32 * 1024 * 1024)
    x = jnp.transpose(column_state, (1, 2, 0))
    span_row = span_of.reshape(1, COL)
    cloud_row = cloud_levels.reshape(1, SLOT)
    hbm = pl.BlockSpec(memory_space=pltpu.HBM)
    message, slots = pl.pallas_call(
        pack_kernel,
        out_shape=(shape((SLOT * CHUNKS, 128), f32), shape((8, SLOT), jnp.int32)),
        in_specs=[hbm] * 6,
        scratch_shapes=[
            pltpu.VMEM((NF, COL, LEV), f32),
            pltpu.VMEM((1, COL), jnp.int32),
            pltpu.VMEM((LEV, SLOT), f32),
            pltpu.VMEM((LEV, SLOT), f32),
            pltpu.VMEM((1, SLOT), jnp.int32),
            pltpu.VMEM((4, 4), jnp.int32),
            pltpu.SemaphoreType.DMA((6,)),
        ],
        compiler_params=params,
        name="pack",
    )(*(in_hbm(a) for a in (x, span_row, diffusivity, courant, cloud_row, neighbors)))
    turned = pl.pallas_call(
        turn_kernel,
        out_shape=shape((PAIR * LEV, 128), f32),
        in_specs=[hbm],
        scratch_shapes=[pltpu.VMEM((NF, COL, LEV), f32), pltpu.SemaphoreType.DMA((1,))],
        compiler_params=params,
        name="turn",
    )(in_hbm(x))
    received = lax.all_to_all(
        message.reshape(SPANS, 16, 128), "curve", split_axis=0, concat_axis=0, tiled=True
    ).reshape(SLOT * CHUNKS, 128)
    half = shape((PAIR * LEV // 2, 128), f32)
    whole = shape((PAIR * LEV, 128), f32)
    physics, near_cut, far_cut = pl.pallas_call(
        element_kernel,
        out_shape=(whole, half, half),
        scratch_shapes=[
            pltpu.VMEM((LEV, 128), f32),
            pltpu.VMEM((LEV, 128), f32),
            pltpu.VMEM((1, LEV, PAIR, 128), f32),
            pltpu.VMEM((LEV, PAIR, 128), f32),
        ],
        compiler_params=params,
        name="element",
    )(received, slots, turned)
    across = swap(physics, lambda i: i + 1 if i % 2 else i - 1)
    chip = swap(physics, lambda i: i ^ 1)
    far = swap(far_cut, lambda i: i + 2 if i // 2 % 2 else i - 2)
    near = swap(near_cut, lambda i: i - 2 if i // 2 % 2 else i + 2)
    span_state, matrix, cut, total = pl.pallas_call(
        span_kernel,
        out_shape=(
            shape((STATE, SLOT), f32), shape((384, 256), bf16), shape((2, 256, 256), bf16), whole
        ),
        scratch_shapes=[
            pltpu.VMEM(((CHUNKS - 1) * 128, 128), f32),
            pltpu.VMEM((LEV, 128), f32),
            pltpu.VMEM((2, LEV, PAIR, 128), f32),
            pltpu.VMEM((LEV, PAIR, 128), f32),
        ],
        compiler_params=params,
        name="span",
    )(received, diffusivity, courant, cloud_row, jnp.asarray(lap_columns), physics)
    total = pl.pallas_call(
        beside_kernel,
        out_shape=whole,
        compiler_params=params,
        name="beside",
    )(across, chip, total, matrix)
    dynamics = pl.pallas_call(
        beyond_kernel,
        out_shape=shape((NF, COL, LEV), f32),
        out_specs=hbm,
        scratch_shapes=[pltpu.VMEM((NF, COL, LEV), f32), pltpu.SemaphoreType.DMA((NF,))],
        compiler_params=params,
        name="beyond",
    )(far, near, total, cut)
    return (
        jnp.transpose(span_state.reshape(NF, LEV, SLOT), (1, 0, 2)),
        jnp.transpose(dynamics, (2, 0, 1)),
    )


def solution(mesh):
    placed = (
        P(None, "field", "curve"),
        P("curve"),
        P(None, "curve"),
        P(None, "curve"),
        P("curve"),
        P(None, "curve"),
    )
    return jax.shard_map(
        per_device,
        mesh=mesh,
        in_specs=placed,
        out_specs=(P(None, "field", "curve"), P(None, "field", "curve")),
        check_vma=False,
    )
```

```python
import numpy as np
import jax
import jax.numpy as jnp
from jax import lax
from jax.experimental import pallas as pl
from jax.experimental.pallas import tpu as pltpu
from jax.sharding import PartitionSpec as P

LEV = 72
HALF = LEV // 2
NF = 12
PAIR = NF // 2
COL = 64
SLOT = 128
WORDS = 1024
CHUNKS = WORDS // 128
STATE = NF * LEV
SPANS = 64
viscosity = 0.02

second_diff = np.array(
    [[-1.0, 1.0, 0.0, 0.0], [1.0, -2.0, 1.0, 0.0], [0.0, 1.0, -2.0, 1.0], [0.0, 0.0, 1.0, -1.0]]
)
lap_nodes = np.kron(np.eye(4), second_diff) + np.kron(second_diff, np.eye(4))
lap_columns = np.kron(lap_nodes, np.eye(4)).astype(np.float32)

f32 = jnp.float32
bf16 = jnp.bfloat16


def iota(shape, axis):
    return lax.broadcasted_iota(jnp.int32, shape, axis)


def split3(x):
    hi = x.astype(bf16)
    rest = x - hi.astype(f32)
    mid = rest.astype(bf16)
    lo = (rest - mid.astype(f32)).astype(bf16)
    return hi, mid, lo


def split2(x):
    hi = x.astype(bf16)
    return hi, (x - hi.astype(f32)).astype(bf16)


def dot(a, b):
    return jnp.dot(a, b, preferred_element_type=f32)


def slots_of(span_row):
    row = span_row.astype(f32)
    square = jnp.broadcast_to(row, (COL, COL))
    column = jnp.sum(
        jnp.where(iota((COL, COL), 0) == iota((COL, COL), 1), square, 0.0), axis=1, keepdims=True
    )
    earlier = jnp.logical_and(column == square, iota((COL, COL), 0) < iota((COL, COL), 1))
    rank = jnp.sum(jnp.where(earlier, 1.0, 0.0), axis=0, keepdims=True)
    return (2.0 * row + rank).astype(jnp.int32)


def active_rate(courant, cloud_row):
    level = iota((LEV, SLOT), 0)
    return jnp.where(level >= LEV - cloud_row, courant, 0.0)


def fetch(sources, targets, sems):
    copies = [
        pltpu.make_async_copy(source, target, sems.at[i])
        for i, (source, target) in enumerate(zip(sources, targets))
    ]
    for copy in copies:
        copy.start()
    return copies


def pack_kernel(
    x_hbm, span_hbm, diff_hbm, courant_hbm, cloud_hbm, near_hbm, out_ref, slot_ref, turned_ref,
    x_ref, span_ref, diff_ref, courant_ref, cloud_ref, near_ref, sems,
):
    copies = fetch(
        (span_hbm, cloud_hbm, near_hbm, diff_hbm, courant_hbm, x_hbm),
        (span_ref, cloud_ref, near_ref, diff_ref, courant_ref, x_ref),
        sems,
    )
    for copy in copies[:5]:
        copy.wait()
    slot_row = slots_of(span_ref[...])
    slot_ref[...] = jnp.broadcast_to(jnp.concatenate([slot_row, slot_row], axis=1), (8, SLOT))
    pick = (iota((SLOT, COL), 0) == slot_row).astype(f32).astype(bf16)
    diff_t = diff_ref[...].T
    rate_t = active_rate(courant_ref[...], cloud_ref[...]).T
    near = near_ref[...].astype(f32)
    near_row = jnp.concatenate([near[s : s + 1, :] for s in range(4)], axis=1)
    near_t = jnp.broadcast_to(near_row, (SLOT, 16))
    copies[5].wait()
    state = jnp.concatenate([x_ref[f] for f in range(NF)], axis=1)
    hi, mid, lo = split3(state)
    packed = dot(pick, hi) + dot(pick, mid) + dot(pick, lo)
    message = jnp.concatenate([packed, diff_t, rate_t, near_t], axis=1)
    for k in range(CHUNKS):
        out_ref[pl.ds(k, SLOT, stride=CHUNKS), :] = message[:, 128 * k : 128 * k + 128]
    for f in range(PAIR):
        both = jnp.concatenate([x_ref[f], x_ref[f + PAIR]], axis=0)
        turned_ref[pl.ds(f * LEV, LEV), :] = both.T


def chunk_t(recv_ref, k):
    return recv_ref[pl.ds(k, SLOT, stride=CHUNKS), :].T


def solve(coef_ref, rate_ref, groups, part_ref, ratio_ref):
    rows = (PAIR, 128)
    zero = jnp.zeros(rows, f32)

    def row(ref, k):
        return jnp.broadcast_to(ref[pl.ds(k, 1), :], rows)

    count = len(groups)
    top_ratio, bot_ratio = zero, zero
    top_part, bot_part = [zero] * count, [zero] * count
    top_flux = [zero] * count
    top_above = zero
    bot_below = row(coef_ref, LEV - 1)
    last = row(rate_ref, LEV - 1)
    bot_state = [load(LEV - 1) for load, _ in groups]
    bot_flux = [last * x for x in bot_state]
    for i in range(HALF):
        t, u = i, LEV - 1 - i
        top_next = row(coef_ref, t)
        bot_next = row(coef_ref, u - 1)
        top_inv = 1.0 / (1.0 + top_above + top_next - top_above * top_ratio)
        bot_inv = 1.0 / (1.0 + bot_below + bot_next - bot_below * bot_ratio)
        top_ratio = top_next * top_inv
        bot_ratio = bot_next * bot_inv
        ratio_ref[i] = top_ratio
        ratio_ref[HALF + i] = bot_ratio
        top_rate = row(rate_ref, t)
        above_rate = row(rate_ref, u - 1)
        for g, (load, _) in enumerate(groups):
            x = load(t)
            flux = top_rate * x
            settled = x - flux + top_flux[g]
            top_flux[g] = flux
            top_part[g] = (settled + top_above * top_part[g]) * top_inv
            part_ref[g, i] = top_part[g]
            above = load(u - 1)
            above_flux = above_rate * above
            settled = bot_state[g] - bot_flux[g] + above_flux
            bot_state[g] = above
            bot_flux[g] = above_flux
            bot_part[g] = (settled + bot_below * bot_part[g]) * bot_inv
            part_ref[g, HALF + i] = bot_part[g]
        top_above = top_next
        bot_below = bot_next
    meet = 1.0 / (1.0 - top_ratio * bot_ratio)
    top, bot = [], []
    for g, (_, store) in enumerate(groups):
        top.append((top_part[g] + top_ratio * bot_part[g]) * meet)
        bot.append((bot_part[g] + bot_ratio * top_part[g]) * meet)
        store(HALF - 1, top[g])
        store(HALF, bot[g])
    for i in range(HALF - 2, -1, -1):
        top_ratio = ratio_ref[i]
        bot_ratio = ratio_ref[HALF + i]
        for g, (_, store) in enumerate(groups):
            top[g] = part_ref[g, i] + top_ratio * top[g]
            bot[g] = part_ref[g, HALF + i] + bot_ratio * bot[g]
            store(i, top[g])
            store(LEV - 1 - i, bot[g])


def strided(in_ref, out_ref, base):
    def load(level):
        return in_ref[pl.ds(base + level, PAIR, stride=LEV), :]

    def store(level, value):
        out_ref[pl.ds(base + level, PAIR, stride=LEV), :] = value

    return load, store


def element_kernel(
    recv_ref, slot_ref, x_ref, out_ref, near_ref, far_ref, coef_ref, rate_ref, part_ref, ratio_ref
):
    device = lax.axis_index("curve")
    spread = (iota((SLOT, 128), 0) == slot_ref[0:1, :]).astype(f32).astype(bf16)
    tail = jnp.concatenate([chunk_t(recv_ref, CHUNKS - 2), chunk_t(recv_ref, CHUNKS - 1)], axis=0)
    begin = STATE - 128 * (CHUNKS - 2)
    hi, mid, lo = split3(tail[begin : begin + 2 * LEV])
    columns = dot(hi, spread) + dot(mid, spread) + dot(lo, spread)
    coef_ref[...] = columns[:LEV]
    rate_ref[...] = columns[LEV:]
    element, relative = neighbour_lanes(recv_ref, device)
    cuts = []
    for o, beyond in ((2, 4), (0, 0)):
        reach = jnp.zeros((COL, COL), f32)
        for s in range(4):
            reach = reach + edge_entries(element, relative, o, s, COL, 2)
        flags = [relative[o][s][:, :32] == beyond for s in range(4)]
        cuts.append(dot(reach.astype(bf16), corner_choice(flags).astype(bf16)))
    up, down = cuts
    odd = lax.rem(device // 2, 2) == 1
    first, second = jnp.where(odd, down, up), jnp.where(odd, up, down)
    zero = jnp.zeros((COL, 32), f32)
    matrix = jnp.concatenate(
        [
            jnp.concatenate([first, zero, second, zero], axis=1),
            jnp.concatenate([zero, first, zero, second], axis=1),
        ],
        axis=0,
    ).astype(bf16)
    solve(coef_ref, rate_ref, [strided(x_ref, out_ref, 0)], part_ref, ratio_ref)
    hi, lo = split2(out_ref[...])
    cut = dot(hi, matrix) + dot(lo, matrix)
    half = PAIR * LEV // 2
    near_ref[...] = jnp.concatenate([cut[:half, :COL], cut[half:, :COL]], axis=1)
    far_ref[...] = jnp.concatenate([cut[:half, COL:], cut[half:, COL:]], axis=1)


def edge_places():
    lane = iota((1, COL), 1)
    node = lane // 4
    node_row, node_col = node // 4, node % 4
    on_edge = [node_row == 0, node_col == 3, node_row == 3, node_col == 0]
    facing = [node + 12, node - 3, node - 12, node + 3]
    return lane, on_edge, facing


def neighbour_lanes(recv_ref, device):
    word = iota((128, 4 * COL), 0) - (128 - 16)
    place = iota((128, 4 * COL), 1)
    spread = (word == (place // COL) * 4 + place % 4).astype(f32).astype(bf16)
    rows = []
    for o in range(3):
        block = lax.rem(device + (o - 1) + SPANS, SPANS)
        rows.append(recv_ref[pl.ds(block * 16 + CHUNKS - 1, 1), :])
    rows = jnp.concatenate(rows + [jnp.zeros((5, 128), f32)], axis=0)
    near = dot(rows.astype(bf16), spread).astype(jnp.int32)
    far = lax.rem(near // 4 - device + (2 + SPANS), SPANS)
    cut = [slice(s * COL, (s + 1) * COL) for s in range(4)]
    element = [[near[o : o + 1, c] % 4 for c in cut] for o in range(3)]
    relative = [[far[o : o + 1, c] for c in cut] for o in range(3)]
    return element, relative


def edge_entries(element, relative, o, s, rows, only=None):
    lane, on_edge, facing = edge_places()
    target = facing[s] * 4 + element[o][s]
    keep = on_edge[s]
    if only is None:
        target = target + relative[o][s] * COL
    else:
        keep = jnp.logical_and(keep, relative[o][s] == only)
    target = jnp.where(keep, target, -1)
    return jnp.where(iota((rows, COL), 0) == target, 0.5, 0.0)


def corner_choice(flags):
    lane = iota((1, 32), 1)
    j = (lane % 16) // 4
    up, right = j // 2, j % 2
    on_row = jnp.where(up == 0, flags[0].astype(f32), flags[2].astype(f32))
    on_col = jnp.where(right == 0, flags[3].astype(f32), flags[1].astype(f32))
    place = iota((COL, 32), 0)
    same = place % 4 == lane % 4
    node = place // 4
    corner = jnp.where(node == up * 12 + right * 3, 1.0, 0.0)
    side = jnp.where(node == (1 + up) * 4 + right * 3, on_row, 0.0)
    side = side + jnp.where(node == up * 12 + 1 + right, on_col, 0.0)
    return jnp.where(same, jnp.where(lane < 16, corner, side), 0.0)


def twice(block):
    zero = jnp.zeros(block.shape, block.dtype)
    top = jnp.concatenate([block, zero], axis=1)
    return jnp.concatenate([top, jnp.concatenate([zero, block], axis=1)], axis=0)


def halo_matrix(recv_ref, lap_ref, matrix_ref, cut_ref):
    device = lax.axis_index("curve")
    lap = lap_ref[...].astype(bf16)
    element, relative = neighbour_lanes(recv_ref, device)
    lane, on_edge, _ = edge_places()
    edges = sum(jnp.where(edge, 1.0, 0.0) for edge in on_edge)
    source = iota((5 * COL, COL), 0)
    sums = []
    for o in range(3):
        own = source == lane + (o + 1) * COL
        total = jnp.where(own, 1.0 - 0.5 * edges, 0.0)
        for s in range(4):
            total = total + edge_entries(element, relative, o, s, 5 * COL)
        sums.append(total)
    second = dot(sums[1][COL : 4 * COL].astype(bf16), lap).astype(bf16)
    matrix = jnp.zeros((3 * COL, COL), f32)
    inner = []
    for o in range(3):
        inner.append(dot(lap, second[o * COL : (o + 1) * COL]).astype(bf16))
        matrix = matrix + dot(sums[o][COL : 4 * COL].astype(bf16), inner[o])
    matrix = sums[1][COL : 4 * COL] - viscosity * matrix
    core = lax.rem(device, 2)
    for o, place in ((0, 1 + core), (1, 0), (2, 2 - core)):
        halves = [twice(block) for block in split2(matrix[o * COL : (o + 1) * COL])]
        start = pl.multiple_of(place * 128, 128)
        matrix_ref[pl.ds(start, 128), :] = jnp.concatenate(halves, axis=1)
    parts = []
    for o in (0, 2):
        flags = [relative[o][s][:, :32] == 2 for s in range(4)]
        choice = corner_choice(flags).astype(bf16)
        parts.append(
            -viscosity
            * lax.dot_general(
                choice, inner[o], (((0,), (0,)), ((), ())), preferred_element_type=f32
            )
        )
    down, up = parts
    odd = lax.rem(device // 2, 2) == 1
    far, near = jnp.where(odd, up, down), jnp.where(odd, down, up)
    for i, block in enumerate((far, near)):
        for h, half in enumerate(split2(block)):
            cut_ref[h, pl.ds(i * 128, 128), :] = twice(twice(half))


def apply(x, matrix):
    hi, lo = split2(x)
    both = dot(hi, matrix)
    return both[:, :128] + both[:, 128:] + dot(lo, matrix[:, :128])


def span_kernel(
    recv_ref, diff_ref, courant_ref, cloud_ref, lap_ref, own_ref,
    out_ref, matrix_ref, cut_ref, part_sum_ref,
    state_ref, rate_ref, part_ref, ratio_ref,
):
    halo_matrix(recv_ref, lap_ref, matrix_ref, cut_ref)
    rate_ref[...] = active_rate(courant_ref[...], cloud_ref[...])
    for k in range(CHUNKS - 1):
        state_ref[pl.ds(128 * k, 128), :] = chunk_t(recv_ref, k)
    groups = [strided(state_ref, out_ref, g * PAIR * LEV) for g in range(2)]
    solve(diff_ref, rate_ref, groups, part_ref, ratio_ref)
    part_sum_ref[...] = apply(own_ref[...], matrix_ref[pl.ds(0, 128), :])


def beside_kernel(across_ref, chip_ref, part_ref, matrix_ref, out_ref):
    x = jnp.concatenate([across_ref[...], chip_ref[...]], axis=1)
    out_ref[...] = part_ref[...] + apply(x, matrix_ref[pl.ds(128, 256), :])


def beyond_kernel(far_ref, near_ref, part_ref, cut_ref, out_hbm, out_ref, sems):
    hi, lo = split2(jnp.concatenate([far_ref[...], near_ref[...]], axis=1))
    cut = dot(hi, cut_ref[0]) + dot(lo, cut_ref[0]) + dot(hi, cut_ref[1])
    total = part_ref[...] + jnp.concatenate([cut[:, :128], cut[:, 128:]], axis=0)
    copies = []
    for f in range(PAIR):
        turned = total[f * LEV : (f + 1) * LEV].T
        out_ref[f] = turned[:COL]
        out_ref[f + PAIR] = turned[COL:]
        for at in (f, f + PAIR):
            copy = pltpu.make_async_copy(out_ref.at[at], out_hbm.at[at], sems.at[at])
            copy.start()
            copies.append(copy)
    for copy in copies:
        copy.wait()


def swap(x, partner):
    return lax.ppermute(x, "curve", [(i, partner(i) % SPANS) for i in range(SPANS)])


def in_hbm(array):
    return pltpu.with_memory_space_constraint(array, pltpu.HBM)


def per_device(column_state, span_of, diffusivity, courant, cloud_levels, neighbors):
    shape = jax.ShapeDtypeStruct
    params = pltpu.CompilerParams(vmem_limit_bytes=32 * 1024 * 1024)
    x = jnp.transpose(column_state, (1, 2, 0))
    span_row = span_of.reshape(1, COL)
    cloud_row = cloud_levels.reshape(1, SLOT)
    hbm = pl.BlockSpec(memory_space=pltpu.HBM)
    message, slots, turned = pl.pallas_call(
        pack_kernel,
        out_shape=(
            shape((SLOT * CHUNKS, 128), f32),
            shape((8, SLOT), jnp.int32),
            shape((PAIR * LEV, 128), f32),
        ),
        in_specs=[hbm] * 6,
        scratch_shapes=[
            pltpu.VMEM((NF, COL, LEV), f32),
            pltpu.VMEM((1, COL), jnp.int32),
            pltpu.VMEM((LEV, SLOT), f32),
            pltpu.VMEM((LEV, SLOT), f32),
            pltpu.VMEM((1, SLOT), jnp.int32),
            pltpu.VMEM((4, 4), jnp.int32),
            pltpu.SemaphoreType.DMA((6,)),
        ],
        compiler_params=params,
        name="pack",
    )(*(in_hbm(a) for a in (x, span_row, diffusivity, courant, cloud_row, neighbors)))
    received = lax.all_to_all(
        message.reshape(SPANS, 16, 128), "curve", split_axis=0, concat_axis=0, tiled=True
    ).reshape(SLOT * CHUNKS, 128)
    half = shape((PAIR * LEV // 2, 128), f32)
    whole = shape((PAIR * LEV, 128), f32)
    physics, near_cut, far_cut = pl.pallas_call(
        element_kernel,
        out_shape=(whole, half, half),
        scratch_shapes=[
            pltpu.VMEM((LEV, 128), f32),
            pltpu.VMEM((LEV, 128), f32),
            pltpu.VMEM((1, LEV, PAIR, 128), f32),
            pltpu.VMEM((LEV, PAIR, 128), f32),
        ],
        compiler_params=params,
        name="element",
    )(received, slots, turned)
    across = swap(physics, lambda i: i + 1 if i % 2 else i - 1)
    chip = swap(physics, lambda i: i ^ 1)
    far = swap(far_cut, lambda i: i + 2 if i // 2 % 2 else i - 2)
    near = swap(near_cut, lambda i: i - 2 if i // 2 % 2 else i + 2)
    span_state, matrix, cut, total = pl.pallas_call(
        span_kernel,
        out_shape=(
            shape((STATE, SLOT), f32), shape((384, 256), bf16), shape((2, 256, 256), bf16), whole
        ),
        scratch_shapes=[
            pltpu.VMEM(((CHUNKS - 1) * 128, 128), f32),
            pltpu.VMEM((LEV, 128), f32),
            pltpu.VMEM((2, LEV, PAIR, 128), f32),
            pltpu.VMEM((LEV, PAIR, 128), f32),
        ],
        compiler_params=params,
        name="span",
    )(received, diffusivity, courant, cloud_row, jnp.asarray(lap_columns), physics)
    total = pl.pallas_call(
        beside_kernel,
        out_shape=whole,
        compiler_params=params,
        name="beside",
    )(across, chip, total, matrix)
    dynamics = pl.pallas_call(
        beyond_kernel,
        out_shape=shape((NF, COL, LEV), f32),
        out_specs=hbm,
        scratch_shapes=[pltpu.VMEM((NF, COL, LEV), f32), pltpu.SemaphoreType.DMA((NF,))],
        compiler_params=params,
        name="beyond",
    )(far, near, total, cut)
    return (
        jnp.transpose(span_state.reshape(NF, LEV, SLOT), (1, 0, 2)),
        jnp.transpose(dynamics, (2, 0, 1)),
    )


def solution(mesh):
    placed = (
        P(None, "field", "curve"),
        P("curve"),
        P(None, "curve"),
        P(None, "curve"),
        P("curve"),
        P(None, "curve"),
    )
    return jax.shard_map(
        per_device,
        mesh=mesh,
        in_specs=placed,
        out_specs=(P(None, "field", "curve"), P(None, "field", "curve")),
        check_vma=False,
    )
```

```python
import numpy as np
import jax
import jax.numpy as jnp
from jax import lax
from jax.experimental import pallas as pl
from jax.experimental.pallas import tpu as pltpu
from jax.sharding import PartitionSpec as P

LEV = 72
HALF = LEV // 2
NF = 12
PAIR = NF // 2
COL = 64
SLOT = 128
WORDS = 1024
CHUNKS = WORDS // 128
STATE = NF * LEV
SPANS = 64
viscosity = 0.02

second_diff = np.array(
    [[-1.0, 1.0, 0.0, 0.0], [1.0, -2.0, 1.0, 0.0], [0.0, 1.0, -2.0, 1.0], [0.0, 0.0, 1.0, -1.0]]
)
lap_nodes = np.kron(np.eye(4), second_diff) + np.kron(second_diff, np.eye(4))
lap_columns = np.kron(lap_nodes, np.eye(4)).astype(np.float32)

f32 = jnp.float32
bf16 = jnp.bfloat16


def iota(shape, axis):
    return lax.broadcasted_iota(jnp.int32, shape, axis)


def split3(x):
    hi = x.astype(bf16)
    rest = x - hi.astype(f32)
    mid = rest.astype(bf16)
    lo = (rest - mid.astype(f32)).astype(bf16)
    return hi, mid, lo


def split2(x):
    hi = x.astype(bf16)
    return hi, (x - hi.astype(f32)).astype(bf16)


def dot(a, b):
    return jnp.dot(a, b, preferred_element_type=f32)


def slots_of(span_row):
    row = span_row.astype(f32)
    square = jnp.broadcast_to(row, (COL, COL))
    column = jnp.sum(
        jnp.where(iota((COL, COL), 0) == iota((COL, COL), 1), square, 0.0), axis=1, keepdims=True
    )
    earlier = jnp.logical_and(column == square, iota((COL, COL), 0) < iota((COL, COL), 1))
    rank = jnp.sum(jnp.where(earlier, 1.0, 0.0), axis=0, keepdims=True)
    return (2.0 * row + rank).astype(jnp.int32)


def active_rate(courant, cloud_row):
    level = iota((LEV, SLOT), 0)
    return jnp.where(level >= LEV - cloud_row, courant, 0.0)


def fetch(sources, targets, sems):
    copies = [
        pltpu.make_async_copy(source, target, sems.at[i])
        for i, (source, target) in enumerate(zip(sources, targets))
    ]
    for copy in copies:
        copy.start()
    return copies


def pack_kernel(
    x_hbm, span_hbm, diff_hbm, courant_hbm, cloud_hbm, near_hbm, out_ref, slot_ref, turned_ref,
    x_ref, span_ref, diff_ref, courant_ref, cloud_ref, near_ref, sems,
):
    copies = fetch(
        (span_hbm, cloud_hbm, near_hbm, diff_hbm, courant_hbm, x_hbm),
        (span_ref, cloud_ref, near_ref, diff_ref, courant_ref, x_ref),
        sems,
    )
    for copy in copies[:5]:
        copy.wait()
    slot_row = slots_of(span_ref[...])
    slot_ref[...] = jnp.broadcast_to(jnp.concatenate([slot_row, slot_row], axis=1), (8, SLOT))
    pick = (iota((SLOT, COL), 0) == slot_row).astype(f32).astype(bf16)
    diff_t = diff_ref[...].T
    rate_t = active_rate(courant_ref[...], cloud_ref[...]).T
    near = near_ref[...].astype(f32)
    near_row = jnp.concatenate([near[s : s + 1, :] for s in range(4)], axis=1)
    near_t = jnp.broadcast_to(near_row, (SLOT, 16))
    copies[5].wait()
    state = jnp.concatenate([x_ref[f] for f in range(NF)], axis=1)
    packed = dot(
        jnp.concatenate([pick, pick, pick], axis=1), jnp.concatenate(split3(state), axis=0)
    )
    message = jnp.concatenate([packed, diff_t, rate_t, near_t], axis=1)
    for k in range(CHUNKS):
        out_ref[pl.ds(k, SLOT, stride=CHUNKS), :] = message[:, 128 * k : 128 * k + 128]
    for f in range(PAIR):
        both = jnp.concatenate([x_ref[f], x_ref[f + PAIR]], axis=0)
        turned_ref[pl.ds(f * LEV, LEV), :] = both.T


def chunk_t(recv_ref, k):
    return recv_ref[pl.ds(k, SLOT, stride=CHUNKS), :].T


def solve(coef_ref, rate_ref, groups, part_ref, ratio_ref):
    rows = (PAIR, 128)
    zero = jnp.zeros(rows, f32)

    def row(ref, k):
        return jnp.broadcast_to(ref[pl.ds(k, 1), :], rows)

    count = len(groups)
    top_ratio, bot_ratio = zero, zero
    top_part, bot_part = [zero] * count, [zero] * count
    top_flux = [zero] * count
    top_above = zero
    bot_below = row(coef_ref, LEV - 1)
    last = row(rate_ref, LEV - 1)
    bot_state = [load(LEV - 1) for load, _ in groups]
    bot_flux = [last * x for x in bot_state]
    for i in range(HALF):
        t, u = i, LEV - 1 - i
        top_next = row(coef_ref, t)
        bot_next = row(coef_ref, u - 1)
        top_inv = 1.0 / (1.0 + top_above + top_next - top_above * top_ratio)
        bot_inv = 1.0 / (1.0 + bot_below + bot_next - bot_below * bot_ratio)
        top_ratio = top_next * top_inv
        bot_ratio = bot_next * bot_inv
        ratio_ref[i] = top_ratio
        ratio_ref[HALF + i] = bot_ratio
        top_rate = row(rate_ref, t)
        above_rate = row(rate_ref, u - 1)
        for g, (load, _) in enumerate(groups):
            x = load(t)
            flux = top_rate * x
            settled = x - flux + top_flux[g]
            top_flux[g] = flux
            top_part[g] = (settled + top_above * top_part[g]) * top_inv
            part_ref[g, i] = top_part[g]
            above = load(u - 1)
            above_flux = above_rate * above
            settled = bot_state[g] - bot_flux[g] + above_flux
            bot_state[g] = above
            bot_flux[g] = above_flux
            bot_part[g] = (settled + bot_below * bot_part[g]) * bot_inv
            part_ref[g, HALF + i] = bot_part[g]
        top_above = top_next
        bot_below = bot_next
    meet = 1.0 / (1.0 - top_ratio * bot_ratio)
    top, bot = [], []
    for g, (_, store) in enumerate(groups):
        top.append((top_part[g] + top_ratio * bot_part[g]) * meet)
        bot.append((bot_part[g] + bot_ratio * top_part[g]) * meet)
        store(HALF - 1, top[g])
        store(HALF, bot[g])
    for i in range(HALF - 2, -1, -1):
        top_ratio = ratio_ref[i]
        bot_ratio = ratio_ref[HALF + i]
        for g, (_, store) in enumerate(groups):
            top[g] = part_ref[g, i] + top_ratio * top[g]
            bot[g] = part_ref[g, HALF + i] + bot_ratio * bot[g]
            store(i, top[g])
            store(LEV - 1 - i, bot[g])


def strided(in_ref, out_ref, base):
    def load(level):
        return in_ref[pl.ds(base + level, PAIR, stride=LEV), :]

    def store(level, value):
        out_ref[pl.ds(base + level, PAIR, stride=LEV), :] = value

    return load, store


def element_kernel(
    recv_ref, slot_ref, x_ref, out_ref, near_ref, far_ref, coef_ref, rate_ref, part_ref, ratio_ref
):
    device = lax.axis_index("curve")
    spread = (iota((SLOT, 128), 0) == slot_ref[0:1, :]).astype(f32).astype(bf16)
    tail = jnp.concatenate([chunk_t(recv_ref, CHUNKS - 2), chunk_t(recv_ref, CHUNKS - 1)], axis=0)
    begin = STATE - 128 * (CHUNKS - 2)
    hi, mid, lo = split3(tail[begin : begin + 2 * LEV])
    columns = dot(hi, spread) + dot(mid, spread) + dot(lo, spread)
    coef_ref[...] = columns[:LEV]
    rate_ref[...] = columns[LEV:]
    element, relative = neighbour_lanes(recv_ref, device)
    cuts = []
    for o, beyond in ((2, 4), (0, 0)):
        reach = jnp.zeros((COL, COL), f32)
        for s in range(4):
            reach = reach + edge_entries(element, relative, o, s, COL, 2)
        flags = [relative[o][s][:, :32] == beyond for s in range(4)]
        cuts.append(dot(reach.astype(bf16), corner_choice(flags).astype(bf16)))
    up, down = cuts
    odd = lax.rem(device // 2, 2) == 1
    first, second = jnp.where(odd, down, up), jnp.where(odd, up, down)
    near, far = twice(first), twice(second)
    zero = jnp.zeros(near.shape, f32)
    upper = jnp.concatenate([near, zero, far, zero], axis=1)
    lower = jnp.concatenate([zero, near, zero, far], axis=1)
    matrix = jnp.concatenate([upper, lower], axis=0).astype(bf16)
    solve(coef_ref, rate_ref, [strided(x_ref, out_ref, 0)], part_ref, ratio_ref)
    half = PAIR * LEV // 2
    hi, lo = split2(jnp.concatenate([out_ref[:half, :], out_ref[half:, :]], axis=1))
    cut = dot(hi, matrix) + dot(lo, matrix)
    near_ref[...] = cut[:, :128]
    far_ref[...] = cut[:, 128:]


def edge_places():
    lane = iota((1, COL), 1)
    node = lane // 4
    node_row, node_col = node // 4, node % 4
    on_edge = [node_row == 0, node_col == 3, node_row == 3, node_col == 0]
    facing = [node + 12, node - 3, node - 12, node + 3]
    return lane, on_edge, facing


def neighbour_lanes(recv_ref, device):
    word = iota((128, 4 * COL), 0) - (128 - 16)
    place = iota((128, 4 * COL), 1)
    spread = (word == (place // COL) * 4 + place % 4).astype(f32).astype(bf16)
    rows = []
    for o in range(3):
        block = lax.rem(device + (o - 1) + SPANS, SPANS)
        rows.append(recv_ref[pl.ds(block * 16 + CHUNKS - 1, 1), :])
    rows = jnp.concatenate(rows + [jnp.zeros((5, 128), f32)], axis=0)
    near = dot(rows.astype(bf16), spread).astype(jnp.int32)
    far = lax.rem(near // 4 - device + (2 + SPANS), SPANS)
    cut = [slice(s * COL, (s + 1) * COL) for s in range(4)]
    element = [[near[o : o + 1, c] % 4 for c in cut] for o in range(3)]
    relative = [[far[o : o + 1, c] for c in cut] for o in range(3)]
    return element, relative


def edge_entries(element, relative, o, s, rows, only=None):
    lane, on_edge, facing = edge_places()
    target = facing[s] * 4 + element[o][s]
    keep = on_edge[s]
    if only is None:
        target = target + relative[o][s] * COL
    else:
        keep = jnp.logical_and(keep, relative[o][s] == only)
    target = jnp.where(keep, target, -1)
    return jnp.where(iota((rows, COL), 0) == target, 0.5, 0.0)


def corner_choice(flags):
    lane = iota((1, 32), 1)
    j = (lane % 16) // 4
    up, right = j // 2, j % 2
    on_row = jnp.where(up == 0, flags[0].astype(f32), flags[2].astype(f32))
    on_col = jnp.where(right == 0, flags[3].astype(f32), flags[1].astype(f32))
    place = iota((COL, 32), 0)
    same = place % 4 == lane % 4
    node = place // 4
    corner = jnp.where(node == up * 12 + right * 3, 1.0, 0.0)
    side = jnp.where(node == (1 + up) * 4 + right * 3, on_row, 0.0)
    side = side + jnp.where(node == up * 12 + 1 + right, on_col, 0.0)
    return jnp.where(same, jnp.where(lane < 16, corner, side), 0.0)


def twice(block):
    zero = jnp.zeros(block.shape, block.dtype)
    top = jnp.concatenate([block, zero], axis=1)
    return jnp.concatenate([top, jnp.concatenate([zero, block], axis=1)], axis=0)


def halo_matrix(recv_ref, lap_ref, matrix_ref, cut_ref):
    device = lax.axis_index("curve")
    lap = lap_ref[...].astype(bf16)
    element, relative = neighbour_lanes(recv_ref, device)
    lane, on_edge, _ = edge_places()
    edges = sum(jnp.where(edge, 1.0, 0.0) for edge in on_edge)
    source = iota((5 * COL, COL), 0)
    sums = []
    for o in range(3):
        own = source == lane + (o + 1) * COL
        total = jnp.where(own, 1.0 - 0.5 * edges, 0.0)
        for s in range(4):
            total = total + edge_entries(element, relative, o, s, 5 * COL)
        sums.append(total)
    second = dot(sums[1][COL : 4 * COL].astype(bf16), lap).astype(bf16)
    matrix = jnp.zeros((3 * COL, COL), f32)
    inner = []
    for o in range(3):
        inner.append(dot(lap, second[o * COL : (o + 1) * COL]).astype(bf16))
        matrix = matrix + dot(sums[o][COL : 4 * COL].astype(bf16), inner[o])
    matrix = sums[1][COL : 4 * COL] - viscosity * matrix
    core = lax.rem(device, 2)
    for o, place in ((0, 1 + core), (1, 0), (2, 2 - core)):
        halves = [twice(block) for block in split2(matrix[o * COL : (o + 1) * COL])]
        start = pl.multiple_of(place * 128, 128)
        matrix_ref[pl.ds(start, 128), :] = jnp.concatenate(halves, axis=1)
    parts = []
    for o in (0, 2):
        flags = [relative[o][s][:, :32] == 2 for s in range(4)]
        choice = corner_choice(flags).astype(bf16)
        parts.append(
            lax.dot_general(choice, inner[o], (((0,), (0,)), ((), ())), preferred_element_type=f32)
        )
    down, up = parts
    odd = lax.rem(device // 2, 2) == 1
    far, near = jnp.where(odd, up, down), jnp.where(odd, down, up)
    for i, block in enumerate((far, near)):
        cut_ref[pl.ds(i * 128, 128), :] = twice(twice(block.astype(bf16)))


def apply(x, matrix):
    hi, lo = split2(x)
    both = dot(hi, matrix)
    return both[:, :128] + both[:, 128:] + dot(lo, matrix[:, :128])


def span_kernel(
    recv_ref, diff_ref, courant_ref, cloud_ref, lap_ref, own_ref,
    out_ref, matrix_ref, cut_ref, part_sum_ref,
    state_ref, rate_ref, part_ref, ratio_ref,
):
    halo_matrix(recv_ref, lap_ref, matrix_ref, cut_ref)
    rate_ref[...] = active_rate(courant_ref[...], cloud_ref[...])
    for k in range(CHUNKS - 1):
        state_ref[pl.ds(128 * k, 128), :] = chunk_t(recv_ref, k)
    groups = [strided(state_ref, out_ref, g * PAIR * LEV) for g in range(2)]
    solve(diff_ref, rate_ref, groups, part_ref, ratio_ref)
    part_sum_ref[...] = apply(own_ref[...], matrix_ref[pl.ds(0, 128), :])


def beside_kernel(across_ref, chip_ref, part_ref, matrix_ref, out_ref):
    x = jnp.concatenate([across_ref[...], chip_ref[...]], axis=1)
    out_ref[...] = part_ref[...] + apply(x, matrix_ref[pl.ds(128, 256), :])


def beyond_kernel(far_ref, near_ref, part_ref, cut_ref, out_hbm, out_ref, sems):
    hi, lo = split2(jnp.concatenate([far_ref[...], near_ref[...]], axis=1))
    cut = dot(hi, cut_ref[...]) + dot(lo, cut_ref[...])
    total = part_ref[...] - viscosity * jnp.concatenate([cut[:, :128], cut[:, 128:]], axis=0)
    copies = []
    for f in range(PAIR):
        turned = total[f * LEV : (f + 1) * LEV].T
        out_ref[f] = turned[:COL]
        out_ref[f + PAIR] = turned[COL:]
        for at in (f, f + PAIR):
            copy = pltpu.make_async_copy(out_ref.at[at], out_hbm.at[at], sems.at[at])
            copy.start()
            copies.append(copy)
    for copy in copies:
        copy.wait()


def swap(x, partner):
    return lax.ppermute(x, "curve", [(i, partner(i) % SPANS) for i in range(SPANS)])


def in_hbm(array):
    return pltpu.with_memory_space_constraint(array, pltpu.HBM)


def per_device(column_state, span_of, diffusivity, courant, cloud_levels, neighbors):
    shape = jax.ShapeDtypeStruct
    params = pltpu.CompilerParams(vmem_limit_bytes=32 * 1024 * 1024)
    x = jnp.transpose(column_state, (1, 2, 0))
    span_row = span_of.reshape(1, COL)
    cloud_row = cloud_levels.reshape(1, SLOT)
    hbm = pl.BlockSpec(memory_space=pltpu.HBM)
    message, slots, turned = pl.pallas_call(
        pack_kernel,
        out_shape=(
            shape((SLOT * CHUNKS, 128), f32),
            shape((8, SLOT), jnp.int32),
            shape((PAIR * LEV, 128), f32),
        ),
        in_specs=[hbm] * 6,
        scratch_shapes=[
            pltpu.VMEM((NF, COL, LEV), f32),
            pltpu.VMEM((1, COL), jnp.int32),
            pltpu.VMEM((LEV, SLOT), f32),
            pltpu.VMEM((LEV, SLOT), f32),
            pltpu.VMEM((1, SLOT), jnp.int32),
            pltpu.VMEM((4, 4), jnp.int32),
            pltpu.SemaphoreType.DMA((6,)),
        ],
        compiler_params=params,
        name="pack",
    )(*(in_hbm(a) for a in (x, span_row, diffusivity, courant, cloud_row, neighbors)))
    received = lax.all_to_all(
        message.reshape(SPANS, 16, 128), "curve", split_axis=0, concat_axis=0, tiled=True
    ).reshape(SLOT * CHUNKS, 128)
    half = shape((PAIR * LEV // 2, 128), f32)
    whole = shape((PAIR * LEV, 128), f32)
    physics, near_cut, far_cut = pl.pallas_call(
        element_kernel,
        out_shape=(whole, half, half),
        scratch_shapes=[
            pltpu.VMEM((LEV, 128), f32),
            pltpu.VMEM((LEV, 128), f32),
            pltpu.VMEM((1, LEV, PAIR, 128), f32),
            pltpu.VMEM((LEV, PAIR, 128), f32),
        ],
        compiler_params=params,
        name="element",
    )(received, slots, turned)
    across = swap(physics, lambda i: i + 1 if i % 2 else i - 1)
    chip = swap(physics, lambda i: i ^ 1)
    far = swap(far_cut, lambda i: i + 2 if i // 2 % 2 else i - 2)
    near = swap(near_cut, lambda i: i - 2 if i // 2 % 2 else i + 2)
    span_state, matrix, cut, total = pl.pallas_call(
        span_kernel,
        out_shape=(
            shape((STATE, SLOT), f32), shape((384, 256), bf16), shape((256, 256), bf16), whole
        ),
        scratch_shapes=[
            pltpu.VMEM(((CHUNKS - 1) * 128, 128), f32),
            pltpu.VMEM((LEV, 128), f32),
            pltpu.VMEM((2, LEV, PAIR, 128), f32),
            pltpu.VMEM((LEV, PAIR, 128), f32),
        ],
        compiler_params=params,
        name="span",
    )(received, diffusivity, courant, cloud_row, jnp.asarray(lap_columns), physics)
    total = pl.pallas_call(
        beside_kernel,
        out_shape=whole,
        compiler_params=params,
        name="beside",
    )(across, chip, total, matrix)
    dynamics = pl.pallas_call(
        beyond_kernel,
        out_shape=shape((NF, COL, LEV), f32),
        out_specs=hbm,
        scratch_shapes=[pltpu.VMEM((NF, COL, LEV), f32), pltpu.SemaphoreType.DMA((NF,))],
        compiler_params=params,
        name="beyond",
    )(far, near, total, cut)
    return (
        jnp.transpose(span_state.reshape(NF, LEV, SLOT), (1, 0, 2)),
        jnp.transpose(dynamics, (2, 0, 1)),
    )


def solution(mesh):
    placed = (
        P(None, "field", "curve"),
        P("curve"),
        P(None, "curve"),
        P(None, "curve"),
        P("curve"),
        P(None, "curve"),
    )
    return jax.shard_map(
        per_device,
        mesh=mesh,
        in_specs=placed,
        out_specs=(P(None, "field", "curve"), P(None, "field", "curve")),
        check_vma=False,
    )
```

```python
import numpy as np
import jax
import jax.numpy as jnp
from jax import lax
from jax.experimental import pallas as pl
from jax.experimental.pallas import tpu as pltpu
from jax.sharding import PartitionSpec as P

LEV = 72
HALF = LEV // 2
NF = 12
PAIR = NF // 2
COL = 64
SLOT = 128
WORDS = 1024
CHUNKS = WORDS // 128
STATE = NF * LEV
SPANS = 64
viscosity = 0.02

second_diff = np.array(
    [[-1.0, 1.0, 0.0, 0.0], [1.0, -2.0, 1.0, 0.0], [0.0, 1.0, -2.0, 1.0], [0.0, 0.0, 1.0, -1.0]]
)
lap_nodes = np.kron(np.eye(4), second_diff) + np.kron(second_diff, np.eye(4))
lap_columns = np.kron(lap_nodes, np.eye(4)).astype(np.float32)

f32 = jnp.float32
bf16 = jnp.bfloat16


def iota(shape, axis):
    return lax.broadcasted_iota(jnp.int32, shape, axis)


def split3(x):
    hi = x.astype(bf16)
    rest = x - hi.astype(f32)
    mid = rest.astype(bf16)
    lo = (rest - mid.astype(f32)).astype(bf16)
    return hi, mid, lo


def split2(x):
    hi = x.astype(bf16)
    return hi, (x - hi.astype(f32)).astype(bf16)


def dot(a, b):
    return jnp.dot(a, b, preferred_element_type=f32)


def slots_of(span_row):
    row = span_row.astype(f32)
    square = jnp.broadcast_to(row, (COL, COL))
    column = jnp.sum(
        jnp.where(iota((COL, COL), 0) == iota((COL, COL), 1), square, 0.0), axis=1, keepdims=True
    )
    earlier = jnp.logical_and(column == square, iota((COL, COL), 0) < iota((COL, COL), 1))
    rank = jnp.sum(jnp.where(earlier, 1.0, 0.0), axis=0, keepdims=True)
    return (2.0 * row + rank).astype(jnp.int32)


def active_rate(courant, cloud_row):
    level = iota((LEV, SLOT), 0)
    return jnp.where(level >= LEV - cloud_row, courant, 0.0)


def fetch(sources, targets, sems):
    copies = [
        pltpu.make_async_copy(source, target, sems.at[i])
        for i, (source, target) in enumerate(zip(sources, targets))
    ]
    for copy in copies:
        copy.start()
    return copies


def pack_kernel(
    x_hbm, span_hbm, diff_hbm, courant_hbm, cloud_hbm, near_hbm, out_ref, slot_ref, turned_ref,
    x_ref, span_ref, diff_ref, courant_ref, cloud_ref, near_ref, sems,
):
    copies = fetch(
        (span_hbm, cloud_hbm, near_hbm, diff_hbm, courant_hbm, x_hbm),
        (span_ref, cloud_ref, near_ref, diff_ref, courant_ref, x_ref),
        sems,
    )
    for copy in copies[:5]:
        copy.wait()
    slot_row = slots_of(span_ref[...])
    slot_ref[...] = jnp.broadcast_to(jnp.concatenate([slot_row, slot_row], axis=1), (8, SLOT))
    pick = (iota((SLOT, COL), 0) == slot_row).astype(f32).astype(bf16)
    diff_t = diff_ref[...].T
    rate_t = active_rate(courant_ref[...], cloud_ref[...]).T
    near = near_ref[...].astype(f32)
    near_row = jnp.concatenate([near[s : s + 1, :] for s in range(4)], axis=1)
    near_t = jnp.broadcast_to(near_row, (SLOT, 16))
    copies[5].wait()
    state = jnp.concatenate([x_ref[f] for f in range(NF)], axis=1)
    packed = dot(
        jnp.concatenate([pick, pick, pick], axis=1), jnp.concatenate(split3(state), axis=0)
    )
    message = jnp.concatenate([packed, diff_t, rate_t, near_t], axis=1)
    for k in range(CHUNKS):
        out_ref[pl.ds(k, SLOT, stride=CHUNKS), :] = message[:, 128 * k : 128 * k + 128]
    for f in range(PAIR):
        both = jnp.concatenate([x_ref[f], x_ref[f + PAIR]], axis=0)
        turned_ref[pl.ds(f * LEV, LEV), :] = both.T


def chunk_t(recv_ref, k):
    return recv_ref[pl.ds(k, SLOT, stride=CHUNKS), :].T


def solve(coef_ref, rate_ref, groups, part_ref, ratio_ref):
    rows = (PAIR, 128)
    zero = jnp.zeros(rows, f32)

    def row(ref, k):
        return jnp.broadcast_to(ref[pl.ds(k, 1), :], rows)

    count = len(groups)
    top_ratio, bot_ratio = zero, zero
    top_part, bot_part = [zero] * count, [zero] * count
    top_flux = [zero] * count
    top_above = zero
    bot_below = row(coef_ref, LEV - 1)
    last = row(rate_ref, LEV - 1)
    bot_state = [load(LEV - 1) for load, _ in groups]
    bot_flux = [last * x for x in bot_state]
    for i in range(HALF):
        t, u = i, LEV - 1 - i
        top_next = row(coef_ref, t)
        bot_next = row(coef_ref, u - 1)
        top_inv = 1.0 / (1.0 + top_above + top_next - top_above * top_ratio)
        bot_inv = 1.0 / (1.0 + bot_below + bot_next - bot_below * bot_ratio)
        top_ratio = top_next * top_inv
        bot_ratio = bot_next * bot_inv
        ratio_ref[i] = top_ratio
        ratio_ref[HALF + i] = bot_ratio
        top_rate = row(rate_ref, t)
        above_rate = row(rate_ref, u - 1)
        for g, (load, _) in enumerate(groups):
            x = load(t)
            flux = top_rate * x
            settled = x - flux + top_flux[g]
            top_flux[g] = flux
            top_part[g] = (settled + top_above * top_part[g]) * top_inv
            part_ref[g, i] = top_part[g]
            above = load(u - 1)
            above_flux = above_rate * above
            settled = bot_state[g] - bot_flux[g] + above_flux
            bot_state[g] = above
            bot_flux[g] = above_flux
            bot_part[g] = (settled + bot_below * bot_part[g]) * bot_inv
            part_ref[g, HALF + i] = bot_part[g]
        top_above = top_next
        bot_below = bot_next
    meet = 1.0 / (1.0 - top_ratio * bot_ratio)
    top, bot = [], []
    for g, (_, store) in enumerate(groups):
        top.append((top_part[g] + top_ratio * bot_part[g]) * meet)
        bot.append((bot_part[g] + bot_ratio * top_part[g]) * meet)
        store(HALF - 1, top[g])
        store(HALF, bot[g])
    for i in range(HALF - 2, -1, -1):
        top_ratio = ratio_ref[i]
        bot_ratio = ratio_ref[HALF + i]
        for g, (_, store) in enumerate(groups):
            top[g] = part_ref[g, i] + top_ratio * top[g]
            bot[g] = part_ref[g, HALF + i] + bot_ratio * bot[g]
            store(i, top[g])
            store(LEV - 1 - i, bot[g])


def strided(in_ref, out_ref, base):
    def load(level):
        return in_ref[pl.ds(base + level, PAIR, stride=LEV), :]

    def store(level, value):
        out_ref[pl.ds(base + level, PAIR, stride=LEV), :] = value

    return load, store


def element_kernel(
    recv_ref, slot_ref, x_ref, out_ref, cut_ref, coef_ref, rate_ref, part_ref, ratio_ref
):
    device = lax.axis_index("curve")
    spread = (iota((SLOT, 128), 0) == slot_ref[0:1, :]).astype(f32).astype(bf16)
    tail = jnp.concatenate([chunk_t(recv_ref, CHUNKS - 2), chunk_t(recv_ref, CHUNKS - 1)], axis=0)
    begin = STATE - 128 * (CHUNKS - 2)
    hi, mid, lo = split3(tail[begin : begin + 2 * LEV])
    columns = dot(hi, spread) + dot(mid, spread) + dot(lo, spread)
    coef_ref[...] = columns[:LEV]
    rate_ref[...] = columns[LEV:]
    element, relative = neighbour_lanes(recv_ref, device)
    cuts = []
    for o, beyond in ((2, 4), (0, 0)):
        reach = jnp.zeros((COL, COL), f32)
        for s in range(4):
            reach = reach + edge_entries(element, relative, o, s, COL, 2)
        flags = [relative[o][s][:, :32] == beyond for s in range(4)]
        cuts.append(dot(reach.astype(bf16), corner_choice(flags).astype(bf16)))
    up, down = cuts
    odd = lax.rem(device // 2, 2) == 1
    first, second = jnp.where(odd, down, up), jnp.where(odd, up, down)
    near, far = twice(first), twice(second)
    zero = jnp.zeros(near.shape, f32)
    upper = jnp.concatenate([near, zero, far, zero], axis=1)
    lower = jnp.concatenate([zero, near, zero, far], axis=1)
    cut_ref[...] = jnp.concatenate([upper, lower], axis=0).astype(bf16)
    solve(coef_ref, rate_ref, [strided(x_ref, out_ref, 0)], part_ref, ratio_ref)


def cut_kernel(x_ref, matrix_ref, near_ref, far_ref):
    half = PAIR * LEV // 2
    hi, lo = split2(jnp.concatenate([x_ref[:half, :], x_ref[half:, :]], axis=1))
    cut = dot(hi, matrix_ref[...]) + dot(lo, matrix_ref[...])
    near_ref[...] = cut[:, :128]
    far_ref[...] = cut[:, 128:]


def edge_places():
    lane = iota((1, COL), 1)
    node = lane // 4
    node_row, node_col = node // 4, node % 4
    on_edge = [node_row == 0, node_col == 3, node_row == 3, node_col == 0]
    facing = [node + 12, node - 3, node - 12, node + 3]
    return lane, on_edge, facing


def neighbour_lanes(recv_ref, device):
    word = iota((128, 4 * COL), 0) - (128 - 16)
    place = iota((128, 4 * COL), 1)
    spread = (word == (place // COL) * 4 + place % 4).astype(f32).astype(bf16)
    rows = []
    for o in range(3):
        block = lax.rem(device + (o - 1) + SPANS, SPANS)
        rows.append(recv_ref[pl.ds(block * 16 + CHUNKS - 1, 1), :])
    rows = jnp.concatenate(rows + [jnp.zeros((5, 128), f32)], axis=0)
    near = dot(rows.astype(bf16), spread).astype(jnp.int32)
    far = lax.rem(near // 4 - device + (2 + SPANS), SPANS)
    cut = [slice(s * COL, (s + 1) * COL) for s in range(4)]
    element = [[near[o : o + 1, c] % 4 for c in cut] for o in range(3)]
    relative = [[far[o : o + 1, c] for c in cut] for o in range(3)]
    return element, relative


def edge_entries(element, relative, o, s, rows, only=None):
    lane, on_edge, facing = edge_places()
    target = facing[s] * 4 + element[o][s]
    keep = on_edge[s]
    if only is None:
        target = target + relative[o][s] * COL
    else:
        keep = jnp.logical_and(keep, relative[o][s] == only)
    target = jnp.where(keep, target, -1)
    return jnp.where(iota((rows, COL), 0) == target, 0.5, 0.0)


def corner_choice(flags):
    lane = iota((1, 32), 1)
    j = (lane % 16) // 4
    up, right = j // 2, j % 2
    on_row = jnp.where(up == 0, flags[0].astype(f32), flags[2].astype(f32))
    on_col = jnp.where(right == 0, flags[3].astype(f32), flags[1].astype(f32))
    place = iota((COL, 32), 0)
    same = place % 4 == lane % 4
    node = place // 4
    corner = jnp.where(node == up * 12 + right * 3, 1.0, 0.0)
    side = jnp.where(node == (1 + up) * 4 + right * 3, on_row, 0.0)
    side = side + jnp.where(node == up * 12 + 1 + right, on_col, 0.0)
    return jnp.where(same, jnp.where(lane < 16, corner, side), 0.0)


def twice(block):
    zero = jnp.zeros(block.shape, block.dtype)
    top = jnp.concatenate([block, zero], axis=1)
    return jnp.concatenate([top, jnp.concatenate([zero, block], axis=1)], axis=0)


def halo_matrix(recv_ref, lap_ref, matrix_ref, cut_ref):
    device = lax.axis_index("curve")
    lap = lap_ref[...].astype(bf16)
    element, relative = neighbour_lanes(recv_ref, device)
    lane, on_edge, _ = edge_places()
    edges = sum(jnp.where(edge, 1.0, 0.0) for edge in on_edge)
    source = iota((5 * COL, COL), 0)
    sums = []
    for o in range(3):
        own = source == lane + (o + 1) * COL
        total = jnp.where(own, 1.0 - 0.5 * edges, 0.0)
        for s in range(4):
            total = total + edge_entries(element, relative, o, s, 5 * COL)
        sums.append(total)
    second = dot(sums[1][COL : 4 * COL].astype(bf16), lap).astype(bf16)
    matrix = jnp.zeros((3 * COL, COL), f32)
    inner = []
    for o in range(3):
        inner.append(dot(lap, second[o * COL : (o + 1) * COL]).astype(bf16))
        matrix = matrix + dot(sums[o][COL : 4 * COL].astype(bf16), inner[o])
    matrix = sums[1][COL : 4 * COL] - viscosity * matrix
    core = lax.rem(device, 2)
    for o, place in ((0, 1 + core), (1, 0), (2, 2 - core)):
        halves = [twice(block) for block in split2(matrix[o * COL : (o + 1) * COL])]
        start = pl.multiple_of(place * 128, 128)
        matrix_ref[pl.ds(start, 128), :] = jnp.concatenate(halves, axis=1)
    parts = []
    for o in (0, 2):
        flags = [relative[o][s][:, :32] == 2 for s in range(4)]
        choice = corner_choice(flags).astype(bf16)
        parts.append(
            lax.dot_general(choice, inner[o], (((0,), (0,)), ((), ())), preferred_element_type=f32)
        )
    down, up = parts
    odd = lax.rem(device // 2, 2) == 1
    far, near = jnp.where(odd, up, down), jnp.where(odd, down, up)
    for i, block in enumerate((far, near)):
        cut_ref[pl.ds(i * 128, 128), :] = twice(twice(block.astype(bf16)))


def apply(x, matrix):
    hi, lo = split2(x)
    both = dot(hi, matrix)
    return both[:, :128] + both[:, 128:] + dot(lo, matrix[:, :128])


def span_kernel(
    recv_ref, diff_ref, courant_ref, cloud_ref, lap_ref, own_ref,
    out_ref, matrix_ref, cut_ref, part_sum_ref,
    state_ref, rate_ref, part_ref, ratio_ref,
):
    halo_matrix(recv_ref, lap_ref, matrix_ref, cut_ref)
    rate_ref[...] = active_rate(courant_ref[...], cloud_ref[...])
    for k in range(CHUNKS - 1):
        state_ref[pl.ds(128 * k, 128), :] = chunk_t(recv_ref, k)
    groups = [strided(state_ref, out_ref, g * PAIR * LEV) for g in range(2)]
    solve(diff_ref, rate_ref, groups, part_ref, ratio_ref)
    part_sum_ref[...] = apply(own_ref[...], matrix_ref[pl.ds(0, 128), :])


def beside_kernel(across_ref, chip_ref, part_ref, matrix_ref, out_ref):
    x = jnp.concatenate([across_ref[...], chip_ref[...]], axis=1)
    out_ref[...] = part_ref[...] + apply(x, matrix_ref[pl.ds(128, 256), :])


def beyond_kernel(far_ref, near_ref, part_ref, cut_ref, out_hbm, out_ref, sems):
    hi, lo = split2(jnp.concatenate([far_ref[...], near_ref[...]], axis=1))
    cut = dot(hi, cut_ref[...]) + dot(lo, cut_ref[...])
    total = part_ref[...] - viscosity * jnp.concatenate([cut[:, :128], cut[:, 128:]], axis=0)
    copies = []
    for f in range(PAIR):
        turned = total[f * LEV : (f + 1) * LEV].T
        out_ref[f] = turned[:COL]
        out_ref[f + PAIR] = turned[COL:]
        for at in (f, f + PAIR):
            copy = pltpu.make_async_copy(out_ref.at[at], out_hbm.at[at], sems.at[at])
            copy.start()
            copies.append(copy)
    for copy in copies:
        copy.wait()


def swap(x, partner):
    return lax.ppermute(x, "curve", [(i, partner(i) % SPANS) for i in range(SPANS)])


def in_hbm(array):
    return pltpu.with_memory_space_constraint(array, pltpu.HBM)


def per_device(column_state, span_of, diffusivity, courant, cloud_levels, neighbors):
    shape = jax.ShapeDtypeStruct
    params = pltpu.CompilerParams(vmem_limit_bytes=32 * 1024 * 1024)
    x = jnp.transpose(column_state, (1, 2, 0))
    span_row = span_of.reshape(1, COL)
    cloud_row = cloud_levels.reshape(1, SLOT)
    hbm = pl.BlockSpec(memory_space=pltpu.HBM)
    message, slots, turned = pl.pallas_call(
        pack_kernel,
        out_shape=(
            shape((SLOT * CHUNKS, 128), f32),
            shape((8, SLOT), jnp.int32),
            shape((PAIR * LEV, 128), f32),
        ),
        in_specs=[hbm] * 6,
        scratch_shapes=[
            pltpu.VMEM((NF, COL, LEV), f32),
            pltpu.VMEM((1, COL), jnp.int32),
            pltpu.VMEM((LEV, SLOT), f32),
            pltpu.VMEM((LEV, SLOT), f32),
            pltpu.VMEM((1, SLOT), jnp.int32),
            pltpu.VMEM((4, 4), jnp.int32),
            pltpu.SemaphoreType.DMA((6,)),
        ],
        compiler_params=params,
        name="pack",
    )(*(in_hbm(a) for a in (x, span_row, diffusivity, courant, cloud_row, neighbors)))
    received = lax.all_to_all(
        message.reshape(SPANS, 16, 128), "curve", split_axis=0, concat_axis=0, tiled=True
    ).reshape(SLOT * CHUNKS, 128)
    half = shape((PAIR * LEV // 2, 128), f32)
    whole = shape((PAIR * LEV, 128), f32)
    physics, cut_matrix = pl.pallas_call(
        element_kernel,
        out_shape=(whole, shape((256, 256), bf16)),
        scratch_shapes=[
            pltpu.VMEM((LEV, 128), f32),
            pltpu.VMEM((LEV, 128), f32),
            pltpu.VMEM((1, LEV, PAIR, 128), f32),
            pltpu.VMEM((LEV, PAIR, 128), f32),
        ],
        compiler_params=params,
        name="element",
    )(received, slots, turned)
    near_cut, far_cut = pl.pallas_call(
        cut_kernel,
        out_shape=(half, half),
        compiler_params=params,
        name="cut",
    )(physics, cut_matrix)
    across = swap(physics, lambda i: i + 1 if i % 2 else i - 1)
    again, near_cut = lax.optimization_barrier((physics, near_cut))
    chip = swap(again, lambda i: i ^ 1)
    far = swap(far_cut, lambda i: i + 2 if i // 2 % 2 else i - 2)
    near = swap(near_cut, lambda i: i - 2 if i // 2 % 2 else i + 2)
    span_state, matrix, cut, total = pl.pallas_call(
        span_kernel,
        out_shape=(
            shape((STATE, SLOT), f32), shape((384, 256), bf16), shape((256, 256), bf16), whole
        ),
        scratch_shapes=[
            pltpu.VMEM(((CHUNKS - 1) * 128, 128), f32),
            pltpu.VMEM((LEV, 128), f32),
            pltpu.VMEM((2, LEV, PAIR, 128), f32),
            pltpu.VMEM((LEV, PAIR, 128), f32),
        ],
        compiler_params=params,
        name="span",
    )(received, diffusivity, courant, cloud_row, jnp.asarray(lap_columns), physics)
    total = pl.pallas_call(
        beside_kernel,
        out_shape=whole,
        compiler_params=params,
        name="beside",
    )(across, chip, total, matrix)
    dynamics = pl.pallas_call(
        beyond_kernel,
        out_shape=shape((NF, COL, LEV), f32),
        out_specs=hbm,
        scratch_shapes=[pltpu.VMEM((NF, COL, LEV), f32), pltpu.SemaphoreType.DMA((NF,))],
        compiler_params=params,
        name="beyond",
    )(far, near, total, cut)
    return (
        jnp.transpose(span_state.reshape(NF, LEV, SLOT), (1, 0, 2)),
        jnp.transpose(dynamics, (2, 0, 1)),
    )


def solution(mesh):
    placed = (
        P(None, "field", "curve"),
        P("curve"),
        P(None, "curve"),
        P(None, "curve"),
        P("curve"),
        P(None, "curve"),
    )
    return jax.shard_map(
        per_device,
        mesh=mesh,
        in_specs=placed,
        out_specs=(P(None, "field", "curve"), P(None, "field", "curve")),
        check_vma=False,
    )
```

```python
import numpy as np
import jax
import jax.numpy as jnp
from jax import lax
from jax.experimental import pallas as pl
from jax.experimental.pallas import tpu as pltpu
from jax.sharding import PartitionSpec as P

LEV = 72
HALF = LEV // 2
NF = 12
PAIR = NF // 2
COL = 64
SLOT = 128
WORDS = 1024
CHUNKS = WORDS // 128
STATE = NF * LEV
SPANS = 64
viscosity = 0.02

second_diff = np.array(
    [[-1.0, 1.0, 0.0, 0.0], [1.0, -2.0, 1.0, 0.0], [0.0, 1.0, -2.0, 1.0], [0.0, 0.0, 1.0, -1.0]]
)
lap_nodes = np.kron(np.eye(4), second_diff) + np.kron(second_diff, np.eye(4))
lap_columns = np.kron(lap_nodes, np.eye(4)).astype(np.float32)

f32 = jnp.float32
bf16 = jnp.bfloat16


def iota(shape, axis):
    return lax.broadcasted_iota(jnp.int32, shape, axis)


def split3(x):
    hi = x.astype(bf16)
    rest = x - hi.astype(f32)
    mid = rest.astype(bf16)
    lo = (rest - mid.astype(f32)).astype(bf16)
    return hi, mid, lo


def split2(x):
    hi = x.astype(bf16)
    return hi, (x - hi.astype(f32)).astype(bf16)


def dot(a, b):
    return jnp.dot(a, b, preferred_element_type=f32)


def slots_of(span_row):
    row = span_row.astype(f32)
    square = jnp.broadcast_to(row, (COL, COL))
    column = jnp.sum(
        jnp.where(iota((COL, COL), 0) == iota((COL, COL), 1), square, 0.0), axis=1, keepdims=True
    )
    earlier = jnp.logical_and(column == square, iota((COL, COL), 0) < iota((COL, COL), 1))
    rank = jnp.sum(jnp.where(earlier, 1.0, 0.0), axis=0, keepdims=True)
    return (2.0 * row + rank).astype(jnp.int32)


def active_rate(courant, cloud_row):
    level = iota((LEV, SLOT), 0)
    return jnp.where(level >= LEV - cloud_row, courant, 0.0)


def fetch(sources, targets, sems):
    copies = [
        pltpu.make_async_copy(source, target, sems.at[i])
        for i, (source, target) in enumerate(zip(sources, targets))
    ]
    for copy in copies:
        copy.start()
    return copies


def pack_kernel(
    x_hbm, span_hbm, diff_hbm, courant_hbm, cloud_hbm, near_hbm, out_ref, slot_ref, turned_ref,
    x_ref, span_ref, diff_ref, courant_ref, cloud_ref, near_ref, sems,
):
    copies = fetch(
        (span_hbm, cloud_hbm, near_hbm, diff_hbm, courant_hbm, x_hbm),
        (span_ref, cloud_ref, near_ref, diff_ref, courant_ref, x_ref),
        sems,
    )
    for copy in copies[:5]:
        copy.wait()
    slot_row = slots_of(span_ref[...])
    slot_ref[...] = jnp.broadcast_to(jnp.concatenate([slot_row, slot_row], axis=1), (8, SLOT))
    pick = (iota((SLOT, COL), 0) == slot_row).astype(f32).astype(bf16)
    diff_t = diff_ref[...].T
    rate_t = active_rate(courant_ref[...], cloud_ref[...]).T
    near = near_ref[...].astype(f32)
    near_row = jnp.concatenate([near[s : s + 1, :] for s in range(4)], axis=1)
    near_t = jnp.broadcast_to(near_row, (SLOT, 16))
    copies[5].wait()
    state = jnp.concatenate([x_ref[f] for f in range(NF)], axis=1)
    packed = dot(
        jnp.concatenate([pick, pick, pick], axis=1), jnp.concatenate(split3(state), axis=0)
    )
    message = jnp.concatenate([packed, diff_t, rate_t, near_t], axis=1)
    for k in range(CHUNKS):
        out_ref[pl.ds(k, SLOT, stride=CHUNKS), :] = message[:, 128 * k : 128 * k + 128]
    for f in range(PAIR):
        both = jnp.concatenate([x_ref[f], x_ref[f + PAIR]], axis=0)
        turned_ref[pl.ds(f * LEV, LEV), :] = both.T


def chunk_t(recv_ref, k):
    return recv_ref[pl.ds(k, SLOT, stride=CHUNKS), :].T


def solve(coef_ref, rate_ref, groups, part_ref, ratio_ref):
    rows = (PAIR, 128)
    zero = jnp.zeros(rows, f32)

    def row(ref, k):
        return jnp.broadcast_to(ref[pl.ds(k, 1), :], rows)

    count = len(groups)
    top_ratio, bot_ratio = zero, zero
    top_part, bot_part = [zero] * count, [zero] * count
    top_flux = [zero] * count
    top_above = zero
    bot_below = row(coef_ref, LEV - 1)
    last = row(rate_ref, LEV - 1)
    bot_state = [load(LEV - 1) for load, _ in groups]
    bot_flux = [last * x for x in bot_state]
    for i in range(HALF):
        t, u = i, LEV - 1 - i
        top_next = row(coef_ref, t)
        bot_next = row(coef_ref, u - 1)
        top_inv = 1.0 / (1.0 + top_above + top_next - top_above * top_ratio)
        bot_inv = 1.0 / (1.0 + bot_below + bot_next - bot_below * bot_ratio)
        top_ratio = top_next * top_inv
        bot_ratio = bot_next * bot_inv
        ratio_ref[i] = top_ratio
        ratio_ref[HALF + i] = bot_ratio
        top_rate = row(rate_ref, t)
        above_rate = row(rate_ref, u - 1)
        for g, (load, _) in enumerate(groups):
            x = load(t)
            flux = top_rate * x
            settled = x - flux + top_flux[g]
            top_flux[g] = flux
            top_part[g] = (settled + top_above * top_part[g]) * top_inv
            part_ref[g, i] = top_part[g]
            above = load(u - 1)
            above_flux = above_rate * above
            settled = bot_state[g] - bot_flux[g] + above_flux
            bot_state[g] = above
            bot_flux[g] = above_flux
            bot_part[g] = (settled + bot_below * bot_part[g]) * bot_inv
            part_ref[g, HALF + i] = bot_part[g]
        top_above = top_next
        bot_below = bot_next
    meet = 1.0 / (1.0 - top_ratio * bot_ratio)
    top, bot = [], []
    for g, (_, store) in enumerate(groups):
        top.append((top_part[g] + top_ratio * bot_part[g]) * meet)
        bot.append((bot_part[g] + bot_ratio * top_part[g]) * meet)
        store(HALF - 1, top[g])
        store(HALF, bot[g])
    for i in range(HALF - 2, -1, -1):
        top_ratio = ratio_ref[i]
        bot_ratio = ratio_ref[HALF + i]
        for g, (_, store) in enumerate(groups):
            top[g] = part_ref[g, i] + top_ratio * top[g]
            bot[g] = part_ref[g, HALF + i] + bot_ratio * bot[g]
            store(i, top[g])
            store(LEV - 1 - i, bot[g])


def strided(in_ref, out_ref, base):
    def load(level):
        return in_ref[pl.ds(base + level, PAIR, stride=LEV), :]

    def store(level, value):
        out_ref[pl.ds(base + level, PAIR, stride=LEV), :] = value

    return load, store


def element_kernel(
    recv_ref, slot_ref, x_ref, out_ref, cut_ref, coef_ref, rate_ref, part_ref, ratio_ref
):
    device = lax.axis_index("curve")
    spread = (iota((SLOT, 128), 0) == slot_ref[0:1, :]).astype(f32).astype(bf16)
    tail = jnp.concatenate(
        [recv_ref[pl.ds(k, SLOT, stride=CHUNKS), :] for k in (CHUNKS - 2, CHUNKS - 1)], axis=1
    )
    begin = STATE - 128 * (CHUNKS - 2)
    columns = dot(
        jnp.concatenate(split3(tail), axis=0).T,
        jnp.concatenate([spread, spread, spread], axis=0),
    )
    coef_ref[...] = columns[begin : begin + LEV]
    rate_ref[...] = columns[begin + LEV : begin + 2 * LEV]
    element, relative = neighbour_lanes(recv_ref, device)
    cuts = []
    for o, beyond in ((2, 4), (0, 0)):
        reach = jnp.zeros((COL, COL), f32)
        for s in range(4):
            reach = reach + edge_entries(element, relative, o, s, COL, 2)
        flags = [relative[o][s][:, :32] == beyond for s in range(4)]
        cuts.append(dot(reach.astype(bf16), corner_choice(flags).astype(bf16)))
    up, down = cuts
    odd = lax.rem(device // 2, 2) == 1
    first, second = jnp.where(odd, down, up), jnp.where(odd, up, down)
    near, far = twice(first), twice(second)
    zero = jnp.zeros(near.shape, f32)
    upper = jnp.concatenate([near, zero, far, zero], axis=1)
    lower = jnp.concatenate([zero, near, zero, far], axis=1)
    cut_ref[...] = jnp.concatenate([upper, lower], axis=0).astype(bf16)
    solve(coef_ref, rate_ref, [strided(x_ref, out_ref, 0)], part_ref, ratio_ref)


def cut_kernel(x_ref, matrix_ref, near_ref, far_ref):
    half = PAIR * LEV // 2
    hi, lo = split2(jnp.concatenate([x_ref[:half, :], x_ref[half:, :]], axis=1))
    cut = dot(hi, matrix_ref[...]) + dot(lo, matrix_ref[...])
    near_ref[...] = cut[:, :128]
    far_ref[...] = cut[:, 128:]


def edge_places():
    lane = iota((1, COL), 1)
    node = lane // 4
    node_row, node_col = node // 4, node % 4
    on_edge = [node_row == 0, node_col == 3, node_row == 3, node_col == 0]
    facing = [node + 12, node - 3, node - 12, node + 3]
    return lane, on_edge, facing


def neighbour_lanes(recv_ref, device):
    word = iota((128, 4 * COL), 0) - (128 - 16)
    place = iota((128, 4 * COL), 1)
    spread = (word == (place // COL) * 4 + place % 4).astype(f32).astype(bf16)
    rows = []
    for o in range(3):
        block = lax.rem(device + (o - 1) + SPANS, SPANS)
        rows.append(recv_ref[pl.ds(block * 16 + CHUNKS - 1, 1), :])
    rows = jnp.concatenate(rows + [jnp.zeros((5, 128), f32)], axis=0)
    near = dot(rows.astype(bf16), spread).astype(jnp.int32)
    far = lax.rem(near // 4 - device + (2 + SPANS), SPANS)
    cut = [slice(s * COL, (s + 1) * COL) for s in range(4)]
    element = [[near[o : o + 1, c] % 4 for c in cut] for o in range(3)]
    relative = [[far[o : o + 1, c] for c in cut] for o in range(3)]
    return element, relative


def edge_entries(element, relative, o, s, rows, only=None):
    lane, on_edge, facing = edge_places()
    target = facing[s] * 4 + element[o][s]
    keep = on_edge[s]
    if only is None:
        target = target + relative[o][s] * COL
    else:
        keep = jnp.logical_and(keep, relative[o][s] == only)
    target = jnp.where(keep, target, -1)
    return jnp.where(iota((rows, COL), 0) == target, 0.5, 0.0)


def corner_choice(flags):
    lane = iota((1, 32), 1)
    j = (lane % 16) // 4
    up, right = j // 2, j % 2
    on_row = jnp.where(up == 0, flags[0].astype(f32), flags[2].astype(f32))
    on_col = jnp.where(right == 0, flags[3].astype(f32), flags[1].astype(f32))
    place = iota((COL, 32), 0)
    same = place % 4 == lane % 4
    node = place // 4
    corner = jnp.where(node == up * 12 + right * 3, 1.0, 0.0)
    side = jnp.where(node == (1 + up) * 4 + right * 3, on_row, 0.0)
    side = side + jnp.where(node == up * 12 + 1 + right, on_col, 0.0)
    return jnp.where(same, jnp.where(lane < 16, corner, side), 0.0)


def twice(block):
    zero = jnp.zeros(block.shape, block.dtype)
    top = jnp.concatenate([block, zero], axis=1)
    return jnp.concatenate([top, jnp.concatenate([zero, block], axis=1)], axis=0)


def halo_matrix(recv_ref, lap_ref, matrix_ref, cut_ref):
    device = lax.axis_index("curve")
    lap = lap_ref[...].astype(bf16)
    element, relative = neighbour_lanes(recv_ref, device)
    lane, on_edge, _ = edge_places()
    edges = sum(jnp.where(edge, 1.0, 0.0) for edge in on_edge)
    source = iota((5 * COL, COL), 0)
    sums = []
    for o in range(3):
        own = source == lane + (o + 1) * COL
        total = jnp.where(own, 1.0 - 0.5 * edges, 0.0)
        for s in range(4):
            total = total + edge_entries(element, relative, o, s, 5 * COL)
        sums.append(total)
    second = dot(sums[1][COL : 4 * COL].astype(bf16), lap).astype(bf16)
    matrix = jnp.zeros((3 * COL, COL), f32)
    inner = []
    for o in range(3):
        inner.append(dot(lap, second[o * COL : (o + 1) * COL]).astype(bf16))
        matrix = matrix + dot(sums[o][COL : 4 * COL].astype(bf16), inner[o])
    matrix = sums[1][COL : 4 * COL] - viscosity * matrix
    core = lax.rem(device, 2)
    for o, place in ((0, 1 + core), (1, 0), (2, 2 - core)):
        halves = [twice(block) for block in split2(matrix[o * COL : (o + 1) * COL])]
        start = pl.multiple_of(place * 128, 128)
        matrix_ref[pl.ds(start, 128), :] = jnp.concatenate(halves, axis=1)
    parts = []
    for o in (0, 2):
        flags = [relative[o][s][:, :32] == 2 for s in range(4)]
        choice = corner_choice(flags).astype(bf16)
        parts.append(
            lax.dot_general(choice, inner[o], (((0,), (0,)), ((), ())), preferred_element_type=f32)
        )
    down, up = parts
    odd = lax.rem(device // 2, 2) == 1
    far, near = jnp.where(odd, up, down), jnp.where(odd, down, up)
    for i, block in enumerate((far, near)):
        cut_ref[pl.ds(i * 128, 128), :] = twice(twice(block.astype(bf16)))


def apply(x, matrix):
    hi, lo = split2(x)
    both = dot(hi, matrix)
    return both[:, :128] + both[:, 128:] + dot(lo, matrix[:, :128])


def span_kernel(
    recv_ref, diff_ref, courant_ref, cloud_ref, lap_ref, own_ref,
    out_ref, matrix_ref, cut_ref, part_sum_ref,
    state_ref, rate_ref, part_ref, ratio_ref,
):
    halo_matrix(recv_ref, lap_ref, matrix_ref, cut_ref)
    rate_ref[...] = active_rate(courant_ref[...], cloud_ref[...])
    for k in range(CHUNKS - 1):
        state_ref[pl.ds(128 * k, 128), :] = chunk_t(recv_ref, k)
    groups = [strided(state_ref, out_ref, g * PAIR * LEV) for g in range(2)]
    solve(diff_ref, rate_ref, groups, part_ref, ratio_ref)
    part_sum_ref[...] = apply(own_ref[...], matrix_ref[pl.ds(0, 128), :])


def beside_kernel(across_ref, chip_ref, part_ref, matrix_ref, out_ref):
    x = jnp.concatenate([across_ref[...], chip_ref[...]], axis=1)
    out_ref[...] = part_ref[...] + apply(x, matrix_ref[pl.ds(128, 256), :])


def beyond_kernel(far_ref, near_ref, part_ref, cut_ref, out_hbm, out_ref, sems):
    hi, lo = split2(jnp.concatenate([far_ref[...], near_ref[...]], axis=1))
    cut = dot(hi, cut_ref[...]) + dot(lo, cut_ref[...])
    total = part_ref[...] - viscosity * jnp.concatenate([cut[:, :128], cut[:, 128:]], axis=0)
    copies = []
    for f in range(PAIR):
        turned = total[f * LEV : (f + 1) * LEV].T
        out_ref[f] = turned[:COL]
        out_ref[f + PAIR] = turned[COL:]
        for at in (f, f + PAIR):
            copy = pltpu.make_async_copy(out_ref.at[at], out_hbm.at[at], sems.at[at])
            copy.start()
            copies.append(copy)
    for copy in copies:
        copy.wait()


def swap(x, partner):
    return lax.ppermute(x, "curve", [(i, partner(i) % SPANS) for i in range(SPANS)])


def in_hbm(array):
    return pltpu.with_memory_space_constraint(array, pltpu.HBM)


def per_device(column_state, span_of, diffusivity, courant, cloud_levels, neighbors):
    shape = jax.ShapeDtypeStruct
    params = pltpu.CompilerParams(vmem_limit_bytes=32 * 1024 * 1024)
    x = jnp.transpose(column_state, (1, 2, 0))
    span_row = span_of.reshape(1, COL)
    cloud_row = cloud_levels.reshape(1, SLOT)
    hbm = pl.BlockSpec(memory_space=pltpu.HBM)
    message, slots, turned = pl.pallas_call(
        pack_kernel,
        out_shape=(
            shape((SLOT * CHUNKS, 128), f32),
            shape((8, SLOT), jnp.int32),
            shape((PAIR * LEV, 128), f32),
        ),
        in_specs=[hbm] * 6,
        scratch_shapes=[
            pltpu.VMEM((NF, COL, LEV), f32),
            pltpu.VMEM((1, COL), jnp.int32),
            pltpu.VMEM((LEV, SLOT), f32),
            pltpu.VMEM((LEV, SLOT), f32),
            pltpu.VMEM((1, SLOT), jnp.int32),
            pltpu.VMEM((4, 4), jnp.int32),
            pltpu.SemaphoreType.DMA((6,)),
        ],
        compiler_params=params,
        name="pack",
    )(*(in_hbm(a) for a in (x, span_row, diffusivity, courant, cloud_row, neighbors)))
    received = lax.all_to_all(
        message.reshape(SPANS, 16, 128), "curve", split_axis=0, concat_axis=0, tiled=True
    ).reshape(SLOT * CHUNKS, 128)
    half = shape((PAIR * LEV // 2, 128), f32)
    whole = shape((PAIR * LEV, 128), f32)
    physics, cut_matrix = pl.pallas_call(
        element_kernel,
        out_shape=(whole, shape((256, 256), bf16)),
        scratch_shapes=[
            pltpu.VMEM((LEV, 128), f32),
            pltpu.VMEM((LEV, 128), f32),
            pltpu.VMEM((1, LEV, PAIR, 128), f32),
            pltpu.VMEM((LEV, PAIR, 128), f32),
        ],
        compiler_params=params,
        name="element",
    )(received, slots, turned)
    near_cut, far_cut = pl.pallas_call(
        cut_kernel,
        out_shape=(half, half),
        compiler_params=params,
        name="cut",
    )(physics, cut_matrix)
    across = swap(physics, lambda i: i + 1 if i % 2 else i - 1)
    again, near_cut = lax.optimization_barrier((physics, near_cut))
    chip = swap(again, lambda i: i ^ 1)
    far = swap(far_cut, lambda i: i + 2 if i // 2 % 2 else i - 2)
    near = swap(near_cut, lambda i: i - 2 if i // 2 % 2 else i + 2)
    span_state, matrix, cut, total = pl.pallas_call(
        span_kernel,
        out_shape=(
            shape((STATE, SLOT), f32), shape((384, 256), bf16), shape((256, 256), bf16), whole
        ),
        scratch_shapes=[
            pltpu.VMEM(((CHUNKS - 1) * 128, 128), f32),
            pltpu.VMEM((LEV, 128), f32),
            pltpu.VMEM((2, LEV, PAIR, 128), f32),
            pltpu.VMEM((LEV, PAIR, 128), f32),
        ],
        compiler_params=params,
        name="span",
    )(received, diffusivity, courant, cloud_row, jnp.asarray(lap_columns), physics)
    total = pl.pallas_call(
        beside_kernel,
        out_shape=whole,
        compiler_params=params,
        name="beside",
    )(across, chip, total, matrix)
    dynamics = pl.pallas_call(
        beyond_kernel,
        out_shape=shape((NF, COL, LEV), f32),
        out_specs=hbm,
        scratch_shapes=[pltpu.VMEM((NF, COL, LEV), f32), pltpu.SemaphoreType.DMA((NF,))],
        compiler_params=params,
        name="beyond",
    )(far, near, total, cut)
    return (
        jnp.transpose(span_state.reshape(NF, LEV, SLOT), (1, 0, 2)),
        jnp.transpose(dynamics, (2, 0, 1)),
    )


def solution(mesh):
    placed = (
        P(None, "field", "curve"),
        P("curve"),
        P(None, "curve"),
        P(None, "curve"),
        P("curve"),
        P(None, "curve"),
    )
    return jax.shard_map(
        per_device,
        mesh=mesh,
        in_specs=placed,
        out_specs=(P(None, "field", "curve"), P(None, "field", "curve")),
        check_vma=False,
    )
```

```python
import numpy as np
import jax
import jax.numpy as jnp
from jax import lax
from jax.experimental import pallas as pl
from jax.experimental.pallas import tpu as pltpu
from jax.sharding import PartitionSpec as P

LEV = 72
HALF = LEV // 2
NF = 12
PAIR = NF // 2
COL = 64
SLOT = 128
WORDS = 1024
CHUNKS = WORDS // 128
STATE = NF * LEV
SPANS = 64
viscosity = 0.02

second_diff = np.array(
    [[-1.0, 1.0, 0.0, 0.0], [1.0, -2.0, 1.0, 0.0], [0.0, 1.0, -2.0, 1.0], [0.0, 0.0, 1.0, -1.0]]
)
lap_nodes = np.kron(np.eye(4), second_diff) + np.kron(second_diff, np.eye(4))
lap_columns = np.kron(lap_nodes, np.eye(4)).astype(np.float32)

f32 = jnp.float32
bf16 = jnp.bfloat16


def iota(shape, axis):
    return lax.broadcasted_iota(jnp.int32, shape, axis)


def split3(x):
    hi = x.astype(bf16)
    rest = x - hi.astype(f32)
    mid = rest.astype(bf16)
    lo = (rest - mid.astype(f32)).astype(bf16)
    return hi, mid, lo


def split2(x):
    hi = x.astype(bf16)
    return hi, (x - hi.astype(f32)).astype(bf16)


def dot(a, b):
    return jnp.dot(a, b, preferred_element_type=f32)


def slots_of(span_row):
    row = span_row.astype(f32)
    square = jnp.broadcast_to(row, (COL, COL))
    column = jnp.sum(
        jnp.where(iota((COL, COL), 0) == iota((COL, COL), 1), square, 0.0), axis=1, keepdims=True
    )
    earlier = jnp.logical_and(column == square, iota((COL, COL), 0) < iota((COL, COL), 1))
    rank = jnp.sum(jnp.where(earlier, 1.0, 0.0), axis=0, keepdims=True)
    return (2.0 * row + rank).astype(jnp.int32)


def active_rate(courant, cloud_row):
    level = iota((LEV, SLOT), 0)
    return jnp.where(level >= LEV - cloud_row, courant, 0.0)


def fetch(sources, targets, sems):
    copies = [
        pltpu.make_async_copy(source, target, sems.at[i])
        for i, (source, target) in enumerate(zip(sources, targets))
    ]
    for copy in copies:
        copy.start()
    return copies


def pack_kernel(
    x_hbm, span_hbm, diff_hbm, courant_hbm, cloud_hbm, near_hbm, out_ref, slot_ref, turned_ref,
    x_ref, span_ref, diff_ref, courant_ref, cloud_ref, near_ref, sems,
):
    copies = fetch(
        (span_hbm, cloud_hbm, near_hbm, diff_hbm, courant_hbm, x_hbm),
        (span_ref, cloud_ref, near_ref, diff_ref, courant_ref, x_ref),
        sems,
    )
    for copy in copies[:5]:
        copy.wait()
    slot_row = slots_of(span_ref[...])
    slot_ref[...] = jnp.broadcast_to(jnp.concatenate([slot_row, slot_row], axis=1), (8, SLOT))
    pick = (iota((SLOT, COL), 0) == slot_row).astype(f32).astype(bf16)
    diff_t = diff_ref[...].T
    rate_t = active_rate(courant_ref[...], cloud_ref[...]).T
    near = near_ref[...].astype(f32)
    near_row = jnp.concatenate([near[s : s + 1, :] for s in range(4)], axis=1)
    near_t = jnp.broadcast_to(near_row, (SLOT, 16))
    copies[5].wait()
    state = jnp.concatenate([x_ref[f] for f in range(NF)], axis=1)
    packed = dot(
        jnp.concatenate([pick, pick, pick], axis=1), jnp.concatenate(split3(state), axis=0)
    )
    message = jnp.concatenate([packed, diff_t, rate_t, near_t], axis=1)
    for k in range(CHUNKS):
        out_ref[pl.ds(k, SLOT, stride=CHUNKS), :] = message[:, 128 * k : 128 * k + 128]
    for f in range(PAIR):
        both = jnp.concatenate([x_ref[f], x_ref[f + PAIR]], axis=0)
        turned_ref[pl.ds(f * LEV, LEV), :] = both.T


def chunk_t(recv_ref, k):
    return recv_ref[pl.ds(k, SLOT, stride=CHUNKS), :].T


def solve(coef_ref, rate_ref, groups, part_ref, ratio_ref):
    rows = (PAIR, 128)
    zero = jnp.zeros(rows, f32)

    def row(ref, k):
        return jnp.broadcast_to(ref[pl.ds(k, 1), :], rows)

    count = len(groups)
    top_ratio, bot_ratio = zero, zero
    top_part, bot_part = [zero] * count, [zero] * count
    top_flux = [zero] * count
    top_above = zero
    bot_below = row(coef_ref, LEV - 1)
    last = row(rate_ref, LEV - 1)
    bot_state = [load(LEV - 1) for load, _ in groups]
    bot_flux = [last * x for x in bot_state]
    for i in range(HALF):
        t, u = i, LEV - 1 - i
        top_next = row(coef_ref, t)
        bot_next = row(coef_ref, u - 1)
        top_inv = 1.0 / (1.0 + top_above + top_next - top_above * top_ratio)
        bot_inv = 1.0 / (1.0 + bot_below + bot_next - bot_below * bot_ratio)
        top_ratio = top_next * top_inv
        bot_ratio = bot_next * bot_inv
        ratio_ref[i] = top_ratio
        ratio_ref[HALF + i] = bot_ratio
        top_rate = row(rate_ref, t)
        above_rate = row(rate_ref, u - 1)
        for g, (load, _) in enumerate(groups):
            x = load(t)
            flux = top_rate * x
            settled = x - flux + top_flux[g]
            top_flux[g] = flux
            top_part[g] = (settled + top_above * top_part[g]) * top_inv
            part_ref[g, i] = top_part[g]
            above = load(u - 1)
            above_flux = above_rate * above
            settled = bot_state[g] - bot_flux[g] + above_flux
            bot_state[g] = above
            bot_flux[g] = above_flux
            bot_part[g] = (settled + bot_below * bot_part[g]) * bot_inv
            part_ref[g, HALF + i] = bot_part[g]
        top_above = top_next
        bot_below = bot_next
    meet = 1.0 / (1.0 - top_ratio * bot_ratio)
    top, bot = [], []
    for g, (_, store) in enumerate(groups):
        top.append((top_part[g] + top_ratio * bot_part[g]) * meet)
        bot.append((bot_part[g] + bot_ratio * top_part[g]) * meet)
        store(HALF - 1, top[g])
        store(HALF, bot[g])
    for i in range(HALF - 2, -1, -1):
        top_ratio = ratio_ref[i]
        bot_ratio = ratio_ref[HALF + i]
        for g, (_, store) in enumerate(groups):
            top[g] = part_ref[g, i] + top_ratio * top[g]
            bot[g] = part_ref[g, HALF + i] + bot_ratio * bot[g]
            store(i, top[g])
            store(LEV - 1 - i, bot[g])


def strided(in_ref, out_ref, base):
    def load(level):
        return in_ref[pl.ds(base + level, PAIR, stride=LEV), :]

    def store(level, value):
        out_ref[pl.ds(base + level, PAIR, stride=LEV), :] = value

    return load, store


def element_kernel(
    recv_ref, slot_ref, x_ref, out_ref, cut_ref, coef_ref, rate_ref, part_ref, ratio_ref
):
    device = lax.axis_index("curve")
    spread = (iota((SLOT, 128), 0) == slot_ref[0:1, :]).astype(f32).astype(bf16)
    tail = jnp.concatenate([chunk_t(recv_ref, CHUNKS - 2), chunk_t(recv_ref, CHUNKS - 1)], axis=0)
    begin = STATE - 128 * (CHUNKS - 2)
    hi, mid, lo = split3(tail[begin : begin + 2 * LEV])
    columns = dot(hi, spread) + dot(mid, spread) + dot(lo, spread)
    coef_ref[...] = columns[:LEV]
    rate_ref[...] = columns[LEV:]
    element, relative = neighbour_lanes(recv_ref, device)
    cuts = []
    for o, beyond in ((2, 4), (0, 0)):
        reach = jnp.zeros((COL, COL), f32)
        for s in range(4):
            reach = reach + edge_entries(element, relative, o, s, COL, 2)
        flags = [relative[o][s][:, :32] == beyond for s in range(4)]
        cuts.append(dot(reach.astype(bf16), corner_choice(flags).astype(bf16)))
    up, down = cuts
    odd = lax.rem(device // 2, 2) == 1
    first, second = jnp.where(odd, down, up), jnp.where(odd, up, down)
    near, far = twice(first), twice(second)
    zero = jnp.zeros(near.shape, f32)
    upper = jnp.concatenate([near, zero, far, zero], axis=1)
    lower = jnp.concatenate([zero, near, zero, far], axis=1)
    cut_ref[...] = jnp.concatenate([upper, lower], axis=0).astype(bf16)
    solve(coef_ref, rate_ref, [strided(x_ref, out_ref, 0)], part_ref, ratio_ref)


def cut_kernel(x_ref, matrix_ref, near_ref, far_ref):
    half = PAIR * LEV // 2
    parts = split2(jnp.concatenate([x_ref[:half, :], x_ref[half:, :]], axis=1))
    matrix = matrix_ref[...]
    cut = dot(jnp.concatenate(parts, axis=1), jnp.concatenate([matrix, matrix], axis=0))
    near_ref[...] = cut[:, :128]
    far_ref[...] = cut[:, 128:]


def edge_places():
    lane = iota((1, COL), 1)
    node = lane // 4
    node_row, node_col = node // 4, node % 4
    on_edge = [node_row == 0, node_col == 3, node_row == 3, node_col == 0]
    facing = [node + 12, node - 3, node - 12, node + 3]
    return lane, on_edge, facing


def neighbour_lanes(recv_ref, device):
    word = iota((128, 4 * COL), 0) - (128 - 16)
    place = iota((128, 4 * COL), 1)
    spread = (word == (place // COL) * 4 + place % 4).astype(f32).astype(bf16)
    rows = []
    for o in range(3):
        block = lax.rem(device + (o - 1) + SPANS, SPANS)
        rows.append(recv_ref[pl.ds(block * 16 + CHUNKS - 1, 1), :])
    rows = jnp.concatenate(rows + [jnp.zeros((5, 128), f32)], axis=0)
    near = dot(rows.astype(bf16), spread).astype(jnp.int32)
    far = lax.rem(near // 4 - device + (2 + SPANS), SPANS)
    cut = [slice(s * COL, (s + 1) * COL) for s in range(4)]
    element = [[near[o : o + 1, c] % 4 for c in cut] for o in range(3)]
    relative = [[far[o : o + 1, c] for c in cut] for o in range(3)]
    return element, relative


def edge_entries(element, relative, o, s, rows, only=None):
    lane, on_edge, facing = edge_places()
    target = facing[s] * 4 + element[o][s]
    keep = on_edge[s]
    if only is None:
        target = target + relative[o][s] * COL
    else:
        keep = jnp.logical_and(keep, relative[o][s] == only)
    target = jnp.where(keep, target, -1)
    return jnp.where(iota((rows, COL), 0) == target, 0.5, 0.0)


def corner_choice(flags):
    lane = iota((1, 32), 1)
    j = (lane % 16) // 4
    up, right = j // 2, j % 2
    on_row = jnp.where(up == 0, flags[0].astype(f32), flags[2].astype(f32))
    on_col = jnp.where(right == 0, flags[3].astype(f32), flags[1].astype(f32))
    place = iota((COL, 32), 0)
    same = place % 4 == lane % 4
    node = place // 4
    corner = jnp.where(node == up * 12 + right * 3, 1.0, 0.0)
    side = jnp.where(node == (1 + up) * 4 + right * 3, on_row, 0.0)
    side = side + jnp.where(node == up * 12 + 1 + right, on_col, 0.0)
    return jnp.where(same, jnp.where(lane < 16, corner, side), 0.0)


def twice(block):
    zero = jnp.zeros(block.shape, block.dtype)
    top = jnp.concatenate([block, zero], axis=1)
    return jnp.concatenate([top, jnp.concatenate([zero, block], axis=1)], axis=0)


def halo_matrix(recv_ref, lap_ref, matrix_ref, cut_ref):
    device = lax.axis_index("curve")
    lap = lap_ref[...].astype(bf16)
    element, relative = neighbour_lanes(recv_ref, device)
    lane, on_edge, _ = edge_places()
    edges = sum(jnp.where(edge, 1.0, 0.0) for edge in on_edge)
    source = iota((5 * COL, COL), 0)
    sums = []
    for o in range(3):
        own = source == lane + (o + 1) * COL
        total = jnp.where(own, 1.0 - 0.5 * edges, 0.0)
        for s in range(4):
            total = total + edge_entries(element, relative, o, s, 5 * COL)
        sums.append(total)
    second = dot(sums[1][COL : 4 * COL].astype(bf16), lap).astype(bf16)
    matrix = jnp.zeros((3 * COL, COL), f32)
    inner = []
    for o in range(3):
        inner.append(dot(lap, second[o * COL : (o + 1) * COL]).astype(bf16))
        matrix = matrix + dot(sums[o][COL : 4 * COL].astype(bf16), inner[o])
    matrix = sums[1][COL : 4 * COL] - viscosity * matrix
    core = lax.rem(device, 2)
    for o, place in ((0, 1 + core), (1, 0), (2, 2 - core)):
        halves = [twice(block) for block in split2(matrix[o * COL : (o + 1) * COL])]
        start = pl.multiple_of(place * 128, 128)
        matrix_ref[pl.ds(start, 128), :] = jnp.concatenate(halves, axis=1)
    parts = []
    for o in (0, 2):
        flags = [relative[o][s][:, :32] == 2 for s in range(4)]
        choice = corner_choice(flags).astype(bf16)
        parts.append(
            lax.dot_general(choice, inner[o], (((0,), (0,)), ((), ())), preferred_element_type=f32)
        )
    down, up = parts
    odd = lax.rem(device // 2, 2) == 1
    far, near = jnp.where(odd, up, down), jnp.where(odd, down, up)
    for i, block in enumerate((far, near)):
        cut_ref[pl.ds(i * 128, 128), :] = twice(twice(block.astype(bf16)))


def apply(x, matrix):
    hi, lo = split2(x)
    both = dot(hi, matrix)
    return both[:, :128] + both[:, 128:] + dot(lo, matrix[:, :128])


def span_kernel(
    recv_ref, diff_ref, courant_ref, cloud_ref, lap_ref, own_ref,
    out_ref, matrix_ref, cut_ref, part_sum_ref,
    state_ref, rate_ref, part_ref, ratio_ref,
):
    halo_matrix(recv_ref, lap_ref, matrix_ref, cut_ref)
    rate_ref[...] = active_rate(courant_ref[...], cloud_ref[...])
    for k in range(CHUNKS - 1):
        state_ref[pl.ds(128 * k, 128), :] = chunk_t(recv_ref, k)
    groups = [strided(state_ref, out_ref, g * PAIR * LEV) for g in range(2)]
    solve(diff_ref, rate_ref, groups, part_ref, ratio_ref)
    part_sum_ref[...] = apply(own_ref[...], matrix_ref[pl.ds(0, 128), :])


def beside_kernel(across_ref, chip_ref, part_ref, matrix_ref, out_ref):
    x = jnp.concatenate([across_ref[...], chip_ref[...]], axis=1)
    out_ref[...] = part_ref[...] + apply(x, matrix_ref[pl.ds(128, 256), :])


def beyond_kernel(far_ref, near_ref, part_ref, cut_ref, out_hbm, out_ref, sems):
    hi, lo = split2(jnp.concatenate([far_ref[...], near_ref[...]], axis=1))
    cut = dot(hi, cut_ref[...]) + dot(lo, cut_ref[...])
    total = part_ref[...] - viscosity * jnp.concatenate([cut[:, :128], cut[:, 128:]], axis=0)
    copies = []
    for f in range(PAIR):
        turned = total[f * LEV : (f + 1) * LEV].T
        out_ref[f] = turned[:COL]
        out_ref[f + PAIR] = turned[COL:]
        for at in (f, f + PAIR):
            copy = pltpu.make_async_copy(out_ref.at[at], out_hbm.at[at], sems.at[at])
            copy.start()
            copies.append(copy)
    for copy in copies:
        copy.wait()


def swap(x, partner):
    return lax.ppermute(x, "curve", [(i, partner(i) % SPANS) for i in range(SPANS)])


def in_hbm(array):
    return pltpu.with_memory_space_constraint(array, pltpu.HBM)


def per_device(column_state, span_of, diffusivity, courant, cloud_levels, neighbors):
    shape = jax.ShapeDtypeStruct
    params = pltpu.CompilerParams(vmem_limit_bytes=32 * 1024 * 1024)
    x = jnp.transpose(column_state, (1, 2, 0))
    span_row = span_of.reshape(1, COL)
    cloud_row = cloud_levels.reshape(1, SLOT)
    hbm = pl.BlockSpec(memory_space=pltpu.HBM)
    message, slots, turned = pl.pallas_call(
        pack_kernel,
        out_shape=(
            shape((SLOT * CHUNKS, 128), f32),
            shape((8, SLOT), jnp.int32),
            shape((PAIR * LEV, 128), f32),
        ),
        in_specs=[hbm] * 6,
        scratch_shapes=[
            pltpu.VMEM((NF, COL, LEV), f32),
            pltpu.VMEM((1, COL), jnp.int32),
            pltpu.VMEM((LEV, SLOT), f32),
            pltpu.VMEM((LEV, SLOT), f32),
            pltpu.VMEM((1, SLOT), jnp.int32),
            pltpu.VMEM((4, 4), jnp.int32),
            pltpu.SemaphoreType.DMA((6,)),
        ],
        compiler_params=params,
        name="pack",
    )(*(in_hbm(a) for a in (x, span_row, diffusivity, courant, cloud_row, neighbors)))
    received = lax.all_to_all(
        message.reshape(SPANS, 16, 128), "curve", split_axis=0, concat_axis=0, tiled=True
    ).reshape(SLOT * CHUNKS, 128)
    half = shape((PAIR * LEV // 2, 128), f32)
    whole = shape((PAIR * LEV, 128), f32)
    physics, cut_matrix = pl.pallas_call(
        element_kernel,
        out_shape=(whole, shape((256, 256), bf16)),
        scratch_shapes=[
            pltpu.VMEM((LEV, 128), f32),
            pltpu.VMEM((LEV, 128), f32),
            pltpu.VMEM((1, LEV, PAIR, 128), f32),
            pltpu.VMEM((LEV, PAIR, 128), f32),
        ],
        compiler_params=params,
        name="element",
    )(received, slots, turned)
    near_cut, far_cut = pl.pallas_call(
        cut_kernel,
        out_shape=(half, half),
        compiler_params=params,
        name="cut",
    )(physics, cut_matrix)
    across = swap(physics, lambda i: i + 1 if i % 2 else i - 1)
    again, near_cut = lax.optimization_barrier((physics, near_cut))
    chip = swap(again, lambda i: i ^ 1)
    far = swap(far_cut, lambda i: i + 2 if i // 2 % 2 else i - 2)
    near = swap(near_cut, lambda i: i - 2 if i // 2 % 2 else i + 2)
    span_state, matrix, cut, total = pl.pallas_call(
        span_kernel,
        out_shape=(
            shape((STATE, SLOT), f32), shape((384, 256), bf16), shape((256, 256), bf16), whole
        ),
        scratch_shapes=[
            pltpu.VMEM(((CHUNKS - 1) * 128, 128), f32),
            pltpu.VMEM((LEV, 128), f32),
            pltpu.VMEM((2, LEV, PAIR, 128), f32),
            pltpu.VMEM((LEV, PAIR, 128), f32),
        ],
        compiler_params=params,
        name="span",
    )(received, diffusivity, courant, cloud_row, jnp.asarray(lap_columns), physics)
    total = pl.pallas_call(
        beside_kernel,
        out_shape=whole,
        compiler_params=params,
        name="beside",
    )(across, chip, total, matrix)
    dynamics = pl.pallas_call(
        beyond_kernel,
        out_shape=shape((NF, COL, LEV), f32),
        out_specs=hbm,
        scratch_shapes=[pltpu.VMEM((NF, COL, LEV), f32), pltpu.SemaphoreType.DMA((NF,))],
        compiler_params=params,
        name="beyond",
    )(far, near, total, cut)
    return (
        jnp.transpose(span_state.reshape(NF, LEV, SLOT), (1, 0, 2)),
        jnp.transpose(dynamics, (2, 0, 1)),
    )


def solution(mesh):
    placed = (
        P(None, "field", "curve"),
        P("curve"),
        P(None, "curve"),
        P(None, "curve"),
        P("curve"),
        P(None, "curve"),
    )
    return jax.shard_map(
        per_device,
        mesh=mesh,
        in_specs=placed,
        out_specs=(P(None, "field", "curve"), P(None, "field", "curve")),
        check_vma=False,
    )
```
